1024 devices in a mesh: node: 64 (over z_hi, x, core), local: 16 (over y, z_lo).
Axes of the slice: x: 8, y: 8, z: 8 (z_hi: 4, z_lo: 2; z = z_hi * 2 + z_lo), core: 2. Of those that a mesh axis runs over, the one named last changes fastest.
Arguments:
- tokens: bfloat16 [5632, 4096], P('local', 'node'), may hold values from -16 to 16
- codes: bfloat16 [4096, 2, 11008], P('local', None, 'node'), may hold values from -1 to 1
- scales: bfloat16 [4096, 2], P('local'), may hold values from 0.0078125 to 0.078125
- cotangent: bfloat16 [5632, 11008], P('local', 'node'), may hold values from -0.079589844 to 0.079589844
Outputs:
- hidden: bfloat16 [5632, 11008], P('local', 'node')
- grads: float32 [4096, 2, 11008], P('local', None, 'node')
The draws below stay inside these ranges and needn't reach their ends.
All inputs are finite; a program needn't handle non-finite values.
Results may differ from the reference program's by a relative error of at most 0.02.
Values may be sent and summed in bfloat16 or wider, within the bound.
A program may use at most 32 MiB of HBM per device.

```python
import math
import jax
import jax.numpy as jnp
from jax import lax

D = 4096
TOK_LOC = 352
BUCKET = 11008
TOKENS = 5632
N_LOCAL = 16


def strengthened(entries, rng, source, target, shards_of, factor):
    owner, partner = [(jnp.arange(entries.shape[position]) // (entries.shape[position] // shards_of)).reshape([-1 if axis == position else 1 for axis in range(entries.ndim)]) for position in (source, target)]
    chosen = jax.random.permutation(rng, shards_of)[partner]
    strong = (owner == chosen) | (owner == (partner + shards_of // 2) % shards_of)
    return jnp.where(strong, factor * entries, entries)


def steps_of(rng, shape, split, least, high):
    def one(axis_at, parts):
        heights = jax.random.uniform(jax.random.fold_in(jax.random.fold_in(rng, 6), axis_at), (parts,), jnp.float32, least / len(split), high / len(split))
        return jnp.repeat(jnp.exp(heights), shape[axis_at] // parts).reshape((-1,) + (1,) * (len(shape) - axis_at - 1))

    gain = one(*split[0])
    for cut in split[1:]:
        gain = gain * one(*cut)
    return gain


def normal_values(stream_key, extent, deviation, reach, split=(), dtype=jnp.bfloat16):
    drawn = jax.random.normal(stream_key, extent, jnp.float32) * deviation
    if len(split) > 0:
        drawn = steps_of(stream_key, extent, split, -0.22, 0.18) * drawn
    return jnp.clip(drawn, min=-reach, max=reach).astype(dtype)


def gaussian_with(key, shape, scale, reach, split, heavy, held_as=jnp.bfloat16):
    array = scale * jax.random.normal(key, shape, jnp.float32)
    if split:
        array = array * steps_of(key, shape, split, -0.22, 0.18)
    return jnp.clip(strengthened(array, jax.random.fold_in(key, 3), *heavy), -reach, reach).astype(held_as)


def setup_inputs(seed: int = 0) -> dict:
    key_of = jax.random.split(jax.random.key(seed), 5)
    tokens = gaussian_with(key_of[0], (TOKENS, D), 1.0, 16.0, ((0, 16), (1, 64)), (0, 1, 64, 4.0))
    codes = jnp.clip(jax.random.uniform(key_of[1], (D, 2, BUCKET), jnp.float32, -1.0, 1.0) * steps_of(key_of[1], (D, 2, BUCKET), ((0, 16), (2, 64)), -0.4, 0.0), -1.0, 1.0).astype(jnp.bfloat16)
    scales = jnp.clip(jnp.exp(math.log(0.078125) - 2.3025851 * jax.random.uniform(key_of[2], (D, 2), jnp.float32) ** steps_of(key_of[2], (D, 2), ((0, 16),), -0.2, 0.2)), 0.0078125, 0.078125).astype(jnp.bfloat16)
    cotangent = normal_values(key_of[3], (TOKENS, BUCKET), (1.0 / (TOK_LOC * N_LOCAL) ** 0.5), 0.079589844, ((0, 16), (1, 64)))
    return {"tokens": tokens, "codes": codes, "scales": scales, "cotangent": cotangent}


def reference(tokens, codes, scales, cotangent):
    rows = codes.shape[0]
    width = codes.shape[2]
    scaled = codes.astype(jnp.float32) * scales.astype(jnp.float32)[:, :, None]
    weights = scaled.astype(jnp.bfloat16).reshape(rows, 2 * width)
    both = jnp.dot(tokens, weights, preferred_element_type=jnp.float32).reshape(tokens.shape[0], 2, width)
    gate = both[:, 0, :]
    up = both[:, 1, :]
    sig = jax.nn.sigmoid(gate)
    silu_gate = gate * sig
    hidden = (silu_gate * up).astype(jnp.bfloat16)
    grad_h = cotangent.astype(jnp.float32)
    dgate = grad_h * up * sig * (1.0 + gate * (1.0 - sig))
    dup = grad_h * silu_gate
    dboth = jnp.stack([dgate, dup], axis=1).astype(jnp.bfloat16).reshape(tokens.shape[0], 2 * width)
    token_blocks = tokens.reshape(N_LOCAL, TOK_LOC, rows)
    grad_blocks = dboth.reshape(N_LOCAL, TOK_LOC, 2 * width)

    def accumulate(total, pieces):
        block_tokens, block_grads = pieces
        term = lax.dot_general(block_tokens, block_grads, (((0,), (0,)), ((), ())), preferred_element_type=jnp.float32)
        return total + term.astype(jnp.bfloat16).astype(jnp.float32), None

    start = jnp.zeros((rows, 2 * width), jnp.float32)
    grads, _ = lax.scan(accumulate, start, (token_blocks, grad_blocks))
    return hidden, grads.reshape(rows, 2, width)
```

```python
import jax
import jax.numpy as jnp
from jax import lax
from jax.experimental import pallas as pl
from jax.experimental.pallas import tpu as pltpu
from jax.sharding import PartitionSpec as P

MESH = pl.DeviceIdType.MESH
F32 = jnp.float32
BF16 = jnp.bfloat16
TOK = 352
FEAT = 64
HALF = 88
ROWS = 2 * HALF
KB = 256
D = 4096
RING = 8

EVENTS = [
    ("a", 1), ("a", 2), ("b", 0, 1), ("o", 1), ("b", 1, 1), ("w",), ("b", -1, 1), ("a", 3), ("a", 4),
    ("b", 2, 1), ("b", -2, 1), ("o", 2), ("b", 0, 2), ("b", 1, 2), ("b", -1, 2), ("b", 3, 1), ("p", 1),
    ("b", -3, 1), ("b", 4, 1), ("b", 2, 2), ("o", 3), ("b", -2, 2), ("b", 0, 3), ("b", 1, 3), ("b", -1, 3),
    ("p", 2), ("b", 3, 2), ("b", -3, 2), ("b", 4, 2), ("o", 4), ("b", 2, 3), ("b", -2, 3), ("b", 0, 4),
    ("b", 1, 4), ("b", -1, 4), ("b", 3, 3), ("p", 3), ("b", -3, 3), ("b", 4, 3), ("b", 2, 4), ("b", -2, 4),
    ("b", 3, 4), ("b", -3, 4), ("b", 4, 4),
]


def kernel(
    tok_ref, w_ref, cot_ref, hid_out, grad_out,
    tt, wb, ct, cot_send, hb, hid_recv, both, dbt, rs_send, rs_recv, fin_send, fin_recv,
    a_s, a_r, b_s, b_r, sib_s, sib_r, y_s, y_r, one_s, one_r, g_s, g_r,
):
    node, local = lax.axis_index("node"), lax.axis_index("local")
    core = node % 2
    x = (node // 2) % 8
    z_lo = local % 2
    z = (node // 16) * 2 + z_lo
    y = local // 2

    def wrap(v):
        return (v + RING) % RING

    def device(cx, cy, cz, cc):
        return ((cz // 2) * 16 + cx * 2 + cc, cy * 2 + cz % 2)

    first, second = jnp.where(core == 0, x, z), jnp.where(core == 0, z, x)

    def at(a, b):
        return jnp.where(core == 0, a, b), jnp.where(core == 0, b, a)

    def on_first(step):
        cx, cz = at(wrap(first + step), second)
        return device(cx, y, cz, core)

    def on_second(step):
        cx, cz = at(first, wrap(second + step))
        return device(cx, y, cz, core)

    def on_y(step):
        return device(x, wrap(y + step), z, core)

    sibling = device(x, y, z, 1 - core)
    partner = device(x, y, (z // 2) * 2 + (1 - z_lo), core)

    def rows_of(a, b, lo=0):
        cx, cz = at(wrap(first + a), wrap(second + b))
        return pl.multiple_of(((cz % 2) * 64 + (cz // 2) * 16 + cx * 2 + core) * FEAT + lo, 16)

    def block(a, b, part=None):
        if part is None:
            return tt.at[pl.ds(rows_of(a, b), FEAT), :]
        return tt.at[pl.ds(rows_of(a, b, 32 * part), 32), :]

    sent = []

    def copy(src, dst, send, recv, target):
        return pltpu.make_async_remote_copy(
            src_ref=src, dst_ref=dst, send_sem=send, recv_sem=recv, device_id=target, device_id_type=MESH
        )

    def send(*args):
        c = copy(*args)
        c.start()
        sent.append(c)

    barrier = pltpu.get_barrier_semaphore()
    peers = [on_first(1), on_first(-1), on_first(2), on_first(-2), on_second(1), on_second(-1), on_y(1), on_y(-1), sibling]
    for peer in peers:
        pl.semaphore_signal(barrier, inc=1, device_id=peer, device_id_type=MESH)

    own = rows_of(0, 0)
    tt[pl.ds(own, FEAT), :] = tok_ref[...]
    mine = 2 * y + z_lo
    theirs = 2 * y + 1 - z_lo
    wb[mine] = w_ref[pl.ds(pl.multiple_of(z_lo * ROWS, 16), ROWS), :]

    def halves(v, width):
        low = v[0:HALF]
        high = jnp.concatenate([v[HALF:172], jnp.zeros((4, width), F32)], axis=0)
        return low, high

    low, high = halves(cot_ref[...].astype(F32), TOK)
    pad = jnp.zeros((8, TOK), F32)
    keep = jnp.where(z_lo == 0, low, high)
    give = jnp.where(z_lo == 0, high, low)
    ct[z_lo] = jnp.concatenate([keep, pad], axis=0).astype(BF16)
    cot_send[...] = jnp.concatenate([give, pad], axis=0).astype(BF16)
    pl.semaphore_wait(barrier, len(peers))

    def a_copy(way, dist):
        sign = 1 - 2 * way
        k = way * 4 + dist - 1
        if dist <= 2:
            src, hops, part = (0, 0), dist, None
        elif dist == 3:
            src, hops, part = (-2 * sign, 0), 1, None
        else:
            src, hops, part = (-2 * sign, 0), 2, way
        ref = block(*src, part)
        return copy(ref, ref, a_s.at[k], a_r.at[k], on_first(sign * hops))

    def a_arrives(way, dist):
        sign = 1 - 2 * way
        k = way * 4 + dist - 1
        ref = block(-sign * dist, 0, way if dist == 4 else None)
        copy(ref, ref, a_s.at[k], a_r.at[k], on_first(sign)).wait_recv()

    def b_index(way, item, step):
        return (way * 8 + item + 3) * 4 + step - 1

    def b_send(way, item, step):
        sign = 1 - 2 * way
        k = b_index(way, item, step)
        ref = block(item, -sign * (step - 1), way if step == 4 else None)
        send(ref, ref, b_s.at[k], b_r.at[k], on_second(sign))

    def b_arrives(way, item, step):
        sign = 1 - 2 * way
        k = b_index(way, item, step)
        ref = block(item, -sign * step, way if step == 4 else None)
        copy(ref, ref, b_s.at[k], b_r.at[k], on_second(sign)).wait_recv()

    def share(a, b):
        k = (a + 3) * 8 + b + 3
        ref = block(a, b)
        send(ref, ref, sib_s.at[k], sib_r.at[k], sibling)

    def y_index(way, kind, step):
        return (way * 2 + kind) * 4 + step - 1

    def y_block(kind, offset):
        return wb.at[2 * wrap(y + offset) + (z_lo if kind == 0 else 1 - z_lo)]

    def y_send(way, kind, step):
        sign = 1 - 2 * way
        k = y_index(way, kind, step)
        ref = y_block(kind, -sign * (step - 1))
        send(ref, ref, y_s.at[k], y_r.at[k], on_y(sign))

    def y_arrives(way, kind, step):
        sign = 1 - 2 * way
        k = y_index(way, kind, step)
        ref = y_block(kind, -sign * step)
        copy(ref, ref, y_s.at[k], y_r.at[k], on_y(sign)).wait_recv()

    def y_steps(way, kind):
        return 4 if way == kind else 3

    for way in range(2):
        for dist in (1, 2):
            c = a_copy(way, dist)
            c.start()
            sent.append(c)
        b_send(way, 0, 1)
        y_send(way, 0, 1)
    w_other = w_ref.at[pl.ds(pl.multiple_of((1 - z_lo) * ROWS, 16), ROWS), :]
    send(w_other, wb.at[mine], one_s.at[0], one_r.at[0], partner)
    share(0, 0)
    send(cot_send, ct.at[z_lo], one_s.at[1], one_r.at[1], partner)

    for event in EVENTS:
        if event[0] == "a":
            dist = event[1]
            for way in range(2):
                a_arrives(way, dist)
                if dist == 2:
                    for far in (3, 4):
                        c = a_copy(way, far)
                        c.start()
                        sent.append(c)
            for item in ((-dist, dist) if dist < 4 else (4,)):
                for way in range(2):
                    b_send(way, item, 1)
                share(item, 0)
        elif event[0] == "b":
            _, item, step = event
            for way in range(2):
                b_arrives(way, item, step)
                if step < 4:
                    b_send(way, item, step + 1)
            if step < 4:
                share(item, -step)
                share(item, step)
            else:
                share(item, 4)
        elif event[0] == "w":
            copy(w_other, wb.at[theirs], one_s.at[0], one_r.at[0], partner).wait_recv()
            for way in range(2):
                y_send(way, 1, 1)
        else:
            kind, step = (0 if event[0] == "o" else 1), event[1]
            for way in range(2):
                if step <= y_steps(way, kind):
                    y_arrives(way, kind, step)
                    if step < y_steps(way, kind):
                        y_send(way, kind, step + 1)
    y_arrives(1, 1, 4)
    copy(cot_send, ct.at[1 - z_lo], one_s.at[1], one_r.at[1], partner).wait_recv()

    def sib_arrives(a, b):
        k = (a + 3) * 8 + b + 3
        cz = jnp.where(core == 0, wrap(z + a), wrap(z + b))
        cx = jnp.where(core == 0, wrap(x + b), wrap(x + a))
        r = pl.multiple_of(((cz % 2) * 64 + (cz // 2) * 16 + cx * 2 + 1 - core) * FEAT, 16)
        ref = tt.at[pl.ds(r, FEAT), :]
        copy(ref, ref, sib_s.at[k], sib_r.at[k], sibling).wait_recv()

    for a in range(-3, 5):
        for b in range(-3, 5):
            sib_arrives(a, b)

    for m in range(2):
        acc = jnp.zeros((ROWS, TOK), F32)
        for k in range(8):
            w = jnp.concatenate([wb[2 * k], wb[2 * k + 1]], axis=1)
            acc += jnp.dot(w, tt[D * m + 512 * k : D * m + 512 * (k + 1), :], preferred_element_type=F32)
        for t in range(3):
            wide = min(128, TOK - 128 * t)
            both[t, :, 0:wide] = acc[:, 128 * t : 128 * t + wide]
        for t in range(3):
            wide = min(128, TOK - 128 * t)
            gate = both[t, pl.ds(0, HALF, stride=2), :][:, 0:wide]
            up = both[t, pl.ds(1, HALF, stride=2), :][:, 0:wide]
            cot = ct[m, :, 128 * t : 128 * t + wide].astype(F32)[0:HALF]
            sig = jax.nn.sigmoid(gate)
            silu = gate * sig
            hid = jnp.concatenate([silu * up, jnp.zeros((8, wide), F32)], axis=0)
            hb[m, :, 128 * t : 128 * t + wide] = hid.astype(BF16)
            both[t, pl.ds(0, HALF, stride=2), 0:wide] = cot * up * sig * (1.0 + gate * (1.0 - sig))
            both[t, pl.ds(1, HALF, stride=2), 0:wide] = cot * silu
            dbt[m, :, 128 * t : 128 * t + wide] = both[t, :, 0:wide].astype(BF16)

    def partial(offset, kind):
        rows = 2 * wrap(y + offset) + (z_lo if kind == 0 else 1 - z_lo)
        off = pl.multiple_of(rows * KB, KB)
        total = jnp.zeros((ROWS, KB), F32)
        for m in range(2):
            total += lax.dot_general(
                dbt[m], tt[pl.ds(D * m + off, KB), :], (((1,), (1,)), ((), ())), preferred_element_type=F32
            )
        return total

    def g_copy(way, kind, step):
        k = y_index(way, kind, step)
        return copy(rs_send.at[k], rs_recv.at[k], g_s.at[k], g_r.at[k], on_y(1 - 2 * way))

    def arrived(way, kind, step):
        g_copy(way, kind, step).wait_recv()
        return rs_recv[y_index(way, kind, step)].astype(F32)

    for step in range(1, 5):
        for way, kind in ((0, 0), (1, 1), (0, 1), (1, 0)):
            steps = y_steps(way, kind)
            if step > steps:
                continue
            total = partial((1 - 2 * way) * (steps + 1 - step), kind)
            if step > 1:
                total += arrived(way, kind, step - 1)
            rs_send[y_index(way, kind, step)] = total.astype(BF16)
            c = g_copy(way, kind, step)
            c.start()
            sent.append(c)
        if step == 1:
            send(hb.at[1 - z_lo], hid_recv, one_s.at[2], one_r.at[2], partner)
    final = partial(0, 1)
    final_own = partial(0, 0)
    final += arrived(0, 1, 3)
    final += arrived(1, 1, 4)
    fin_send[...] = final.astype(BF16)
    send(fin_send, fin_recv, one_s.at[3], one_r.at[3], partner)

    copy(hb.at[1 - z_lo], hid_recv, one_s.at[2], one_r.at[2], partner).wait_recv()
    here = hb[z_lo].astype(F32)
    there = hid_recv[...].astype(F32)
    h_low = jnp.where(z_lo == 0, here, there)[0:HALF]
    h_high = jnp.where(z_lo == 0, there, here)[0 : 172 - HALF]
    hid_out[...] = jnp.concatenate([h_low, h_high], axis=0).astype(BF16)

    final_own += arrived(1, 0, 3)
    final_own += arrived(0, 0, 4)
    copy(fin_send, fin_recv, one_s.at[3], one_r.at[3], partner).wait_recv()
    other = fin_recv[...].astype(F32)
    grad_out[0:ROWS, :] = jnp.where(z_lo == 0, final_own, other)
    grad_out[ROWS:344, :] = jnp.where(z_lo == 0, other, final_own)[0 : 344 - ROWS]
    for c in sent:
        c.wait_send()


def body(tokens, codes, scales, cotangent):
    scaled = jnp.transpose(codes, (2, 1, 0)).astype(F32) * jnp.transpose(scales).astype(F32)[None]
    weights = jnp.pad(scaled.astype(BF16).reshape(344, KB), ((0, 8), (0, 0)))
    dma = pltpu.SemaphoreType.DMA
    vmem = pl.BlockSpec(memory_space=pltpu.VMEM)
    hidden, grads = pl.pallas_call(
        kernel,
        name="glu",
        out_shape=(jax.ShapeDtypeStruct((172, TOK), BF16), jax.ShapeDtypeStruct((344, KB), F32)),
        in_specs=[vmem] * 3,
        out_specs=(vmem, vmem),
        scratch_shapes=[
            pltpu.VMEM((2 * D, TOK), BF16),
            pltpu.VMEM((16, ROWS, KB), BF16),
            pltpu.VMEM((2, 96, TOK), BF16),
            pltpu.VMEM((96, TOK), BF16),
            pltpu.VMEM((2, 96, TOK), BF16),
            pltpu.VMEM((96, TOK), BF16),
            pltpu.VMEM((3, ROWS, 128), F32),
            pltpu.VMEM((2, ROWS, TOK), BF16),
            pltpu.VMEM((16, ROWS, KB), BF16),
            pltpu.VMEM((16, ROWS, KB), BF16),
            pltpu.VMEM((ROWS, KB), BF16),
            pltpu.VMEM((ROWS, KB), BF16),
            dma((8,)), dma((8,)), dma((64,)), dma((64,)), dma((64,)), dma((64,)),
            dma((16,)), dma((16,)), dma((4,)), dma((4,)), dma((16,)), dma((16,)),
        ],
        compiler_params=pltpu.CompilerParams(
            collective_id=0, has_side_effects=True, vmem_limit_bytes=40 * 2**20
        ),
    )(jnp.transpose(tokens), weights, jnp.transpose(cotangent))
    return jnp.transpose(hidden), jnp.transpose(grads.reshape(172, 2, KB), (2, 1, 0))


def solution(mesh):
    in_specs = (P("local", "node"), P("local", None, "node"), P("local", None), P("local", "node"))
    out_specs = (P("local", "node"), P("local", None, "node"))
    return jax.shard_map(body, mesh=mesh, in_specs=in_specs, out_specs=out_specs, check_vma=False)
```

```python
import jax
import jax.numpy as jnp
from jax import lax
from jax.experimental import pallas as pl
from jax.experimental.pallas import tpu as pltpu
from jax.sharding import PartitionSpec as P

MESH = pl.DeviceIdType.MESH
F32 = jnp.float32
BF16 = jnp.bfloat16
TOK = 352
FEAT = 64
HID = 172
HALF = 88
ROWS = 2 * HALF
KB = 256
RING = 8
BLOCK = 176
CUT = 96

FIRST = [
    ("+", "a", 2), ("+", "a", 1), ("+", "b", 0, 1),
]
STEPS = [
    ("-", "a", 2), ("+", "a", 3), ("+", "a", 4), ("+", "b", 2, 1), ("-", "a", 1), ("-", "w", 0), ("+", "b", -2, 1),
    ("-", "w", 1), ("+", "b", 1, 1), ("-", "o", 1, 0), ("+", "b", -1, 1), ("-", "b", 0, 1), ("+", "b", 0, 2),
    ("-", "o", 1, 1), ("-", "a", 3), ("+", "b", 3, 1), ("+", "b", -3, 1), ("-", "a", 4), ("+", "b", 4, 1),
    ("-", "p", 1, 0), ("-", "b", 2, 1), ("+", "b", 2, 2), ("-", "b", -2, 1), ("+", "b", -2, 2), ("-", "p", 1, 1),
    ("-", "b", 1, 1), ("+", "b", 1, 2), ("-", "b", -1, 1), ("+", "b", -1, 2), ("-", "o", 2, 0), ("-", "b", 0, 2),
    ("+", "b", 0, 3), ("-", "b", 3, 1), ("+", "b", 3, 2), ("-", "o", 2, 1), ("-", "b", -3, 1), ("+", "b", -3, 2),
    ("-", "b", 4, 1), ("+", "b", 4, 2), ("-", "p", 2, 0), ("-", "b", 2, 2), ("+", "b", 2, 3), ("-", "b", -2, 2),
    ("+", "b", -2, 3), ("-", "p", 2, 1), ("-", "b", 1, 2), ("+", "b", 1, 3), ("-", "b", -1, 2), ("+", "b", -1, 3),
    ("-", "o", 3, 0), ("-", "b", 0, 3), ("+", "b", 0, 4), ("-", "b", 3, 2), ("+", "b", 3, 3), ("-", "o", 3, 1),
    ("-", "b", -3, 2), ("+", "b", -3, 3), ("-", "b", 4, 2), ("+", "b", 4, 4), ("+", "b", 4, 3), ("-", "p", 3, 0),
    ("-", "b", 2, 3), ("+", "b", 2, 4), ("-", "b", -2, 3), ("+", "b", -2, 4), ("-", "p", 3, 1), ("-", "b", 1, 3),
    ("+", "b", 1, 4), ("-", "b", -1, 3), ("+", "b", -1, 4), ("-", "b", 0, 4), ("-", "o", 4, 0), ("-", "b", 3, 3),
    ("+", "b", 3, 4), ("-", "b", -3, 3), ("+", "b", -3, 4), ("-", "o", 4, 1), ("-", "p", 4, 0), ("-", "b", 4, 4),
    ("-", "b", 4, 3), ("-", "b", 2, 4), ("-", "p", 4, 1), ("-", "b", -2, 4), ("-", "b", 1, 4), ("-", "b", -1, 4),
    ("-", "b", 3, 4), ("-", "b", -3, 4),
]


def kernel(
    tok_hbm, codes_hbm, scales_hbm, cot_hbm, hid_out, grad_out,
    tok, codes, scales, cots, tb, tail, wb, w_other, ct, cot_send, hb, hid_keep, hid_recv, both, dbt, rs_send, rs_recv,
    fin_send, fin_recv, in_sem, out_sem, sent_sem, a_r, b_r, sib_r, y_r, one_r, g_r,
):
    loads = [
        pltpu.make_async_copy(tok_hbm, tok, in_sem.at[0]),
        pltpu.make_async_copy(codes_hbm, codes.at[pl.ds(0, HID)], in_sem.at[1]),
        pltpu.make_async_copy(scales_hbm, scales, in_sem.at[2]),
        pltpu.make_async_copy(cot_hbm, cots, in_sem.at[3]),
    ]
    for c in loads:
        c.start()

    node, local = lax.axis_index("node"), lax.axis_index("local")
    core = lax.rem(node, 2)
    x = lax.rem(lax.div(node, 2), 8)
    z_lo = lax.rem(local, 2)
    z = lax.div(node, 16) * 2 + z_lo
    y = lax.div(local, 2)

    def wrap(v):
        return lax.rem(v + RING, RING)

    def device(cx, cy, cz, cc):
        return (lax.div(cz, 2) * 16 + cx * 2 + cc, cy * 2 + lax.rem(cz, 2))

    first, second = jnp.where(core == 0, x, z), jnp.where(core == 0, z, x)

    def at(a, b):
        return jnp.where(core == 0, a, b), jnp.where(core == 0, b, a)

    def on_first(step):
        cx, cz = at(wrap(first + step), second)
        return device(cx, y, cz, core)

    def on_second(step):
        cx, cz = at(first, wrap(second + step))
        return device(cx, y, cz, core)

    def on_y(step):
        return device(x, wrap(y + step), z, core)

    sibling = device(x, y, z, 1 - core)
    partner = device(x, y, lax.div(z, 2) * 2 + (1 - z_lo), core)

    def block_index(cx, cz, cc):
        return (lax.rem(cz, 2) * 2 + cc) * 32 + lax.div(cz, 2) * 8 + cx

    first_at = {a: wrap(first + a) for a in range(-4, 5)}
    second_at = {b: wrap(second + b) for b in range(-4, 5)}

    def index_of(a, b):
        cx, cz = at(first_at[a], second_at[b])
        return block_index(cx, cz, core)

    def sibling_index(a, b):
        cx, cz = at(first_at[b], second_at[a])
        return block_index(cx, cz, 1 - core)

    def block(index, part=None):
        if part is None:
            return tb.at[index]
        return tb.at[index, pl.ds(0, CUT) if part == 0 else pl.ds(CUT, BLOCK - CUT), :]

    pieces = [0, 0]

    def copy(src, dst, kind, recv_sem, target):
        return pltpu.make_async_remote_copy(
            src_ref=src, dst_ref=dst, send_sem=sent_sem.at[kind], recv_sem=recv_sem, device_id=target,
            device_id_type=MESH,
        )

    def start(c, kind, count=1):
        c.start()
        if kind < 2:
            pieces[kind] += count

    def take(recv_sem, count=1):
        ref = tb.at[pl.ds(0, count)]
        copy(ref, ref, 0, recv_sem, sibling).wait_recv()

    def all_left(kind):
        ref = tb.at[pl.ds(0, round(pieces[kind]))]
        copy(ref, ref, kind, a_r.at[0], sibling).wait_send()

    barrier = pltpu.get_barrier_semaphore()
    peers = [sibling, on_y(1), on_y(-1)]
    for step in (1, -1, 2, -2):
        peers += [on_first(step), on_second(step)]
    for peer in peers:
        pl.semaphore_signal(barrier, inc=1, device_id=peer, device_id_type=MESH)

    own = index_of(0, 0)
    loads[0].wait()
    t = tok[...]
    tb[own, 0:64, :] = t[:, 0:128]
    tb[own, 64:128, :] = t[:, 128:256]
    rest = t[:, 256:352]
    tail[own, :, 0:96] = rest
    r = [rest[16 * i : 16 * i + 16, :] for i in range(4)]
    tb[own, 128:144, :] = jnp.concatenate([r[0], r[1][:, 0:32]], axis=1)
    tb[own, 144:160, :] = jnp.concatenate([r[1][:, 32:96], r[2][:, 0:64]], axis=1)
    tb[own, 160:176, :] = jnp.concatenate([r[2][:, 64:96], r[3]], axis=1)

    codes[HID : 2 * HALF] = jnp.zeros((2 * HALF - HID, 2, KB), BF16)
    loads[1].wait()
    loads[2].wait()
    scale = scales[...].astype(F32)[None]

    def weights(half):
        part = codes[pl.ds(half * HALF, HALF)].astype(F32) * scale
        w = part.reshape(ROWS, KB).astype(BF16)
        return (
            jnp.concatenate([w[:, 0:64], w[:, 128:192]], axis=1),
            jnp.concatenate([w[:, 64:128], w[:, 192:256]], axis=1),
        )

    for h, w in enumerate(weights(1 - z_lo)):
        w_other[h] = w
    pl.semaphore_wait(barrier, len(peers))

    def unpack(q):
        p0, p1, p2 = tb[q, 128:144, :], tb[q, 144:160, :], tb[q, 160:176, :]
        tail[q, 0:16, 0:96] = p0[:, 0:96]
        tail[q, 16:32, 0:96] = jnp.concatenate([p0[:, 96:128], p1[:, 0:64]], axis=1)
        tail[q, 32:48, 0:96] = jnp.concatenate([p1[:, 64:128], p2[:, 0:32]], axis=1)
        tail[q, 48:64, 0:96] = p2[:, 32:128]

    def a_send(way, dist):
        sign = 1 - 2 * way
        if dist <= 2:
            at_a, hops, part = 0, dist, None
        elif dist == 3:
            at_a, hops, part = -2 * sign, 1, None
        else:
            at_a, hops, part = -2 * sign, 2, way
        ref = block(index_of(at_a, 0), part)
        start(copy(ref, ref, 0, a_r.at[dist - 1], on_first(sign * hops)), 0, share_of(dist, way))

    def share_of(step, way):
        return 1 if step < 4 else (CUT if way == 0 else BLOCK - CUT) / BLOCK

    def a_arrives(dist):
        take(a_r.at[dist - 1], 2 if dist < 4 else 1)

    def b_sem(item, step):
        return b_r.at[(item + 3) * 4 + step - 1]

    def b_send(way, item, step):
        sign = 1 - 2 * way
        hops = 2 if (item, step) == (4, 4) else 1
        ref = block(index_of(item, -sign * (step - hops)), way if step == 4 else None)
        start(copy(ref, ref, 0, b_sem(item, step), on_second(sign * hops)), 0, share_of(step, way))

    def b_arrives(item, step):
        take(b_sem(item, step), 2 if step < 4 else 1)

    shared = [[]]
    taken = [0]

    def share(blocks):
        if len(shared[-1]) == 4 or len(shared) == 1 and shared[0] == [(0, 0)]:
            shared.append([])
        for a, b in blocks:
            q = index_of(a, b)
            start(copy(block(q), block(q), 0, sib_r.at[len(shared) - 1], sibling), 0)
            shared[-1].append((a, b))
            if (a, b) != (0, 0):
                unpack(q)

    def take_shared(all_of_them):
        while taken[0] < len(shared) - (0 if all_of_them else 2):
            group = shared[taken[0]]
            take(sib_r.at[taken[0]], len(group))
            for a, b in group:
                unpack(sibling_index(a, b))
            taken[0] += 1

    def y_sem(kind, step, h):
        return y_r.at[(kind * 4 + step - 1) * 2 + h]

    def row_block(kind, offset):
        return 2 * wrap(y + offset) + (z_lo if kind == 0 else 1 - z_lo)

    def y_steps(way, kind):
        return 4 if way == kind else 3

    def y_send(way, kind, step, h):
        sign = 1 - 2 * way
        ref = wb.at[h, row_block(kind, -sign * (step - 1))]
        start(copy(ref, ref, 1, y_sem(kind, step, h), on_y(sign)), 1)

    mine = row_block(0, 0)
    theirs = row_block(1, 0)

    def w_copy(h, dst):
        return copy(w_other.at[h], wb.at[h, dst], 1, one_r.at[h], partner)

    def token_send(what):
        for way in range(2):
            if what[1] == "a":
                a_send(way, what[2])
            else:
                b_send(way, what[2], what[3])

    for what in FIRST:
        token_send(what)
    share([(0, 0)])

    for h in range(2):
        start(w_copy(h, mine), 1)
    for h, w in enumerate(weights(z_lo)):
        wb[h, mine] = w
        for way in range(2):
            y_send(way, 0, 1, h)

    loads[3].wait()
    cot = cots[...].astype(F32)
    low, high = cot[0:HALF], jnp.concatenate([cot[HALF:HID], jnp.zeros((2 * HALF - HID, TOK), F32)], axis=0)
    pad = jnp.zeros((8, TOK), F32)
    ct[z_lo] = jnp.concatenate([jnp.where(z_lo == 0, low, high), pad], axis=0).astype(BF16)
    cot_send[...] = jnp.concatenate([jnp.where(z_lo == 0, high, low), pad], axis=0).astype(BF16)

    for what in STEPS:
        if what[0] == "+":
            token_send(what)
            if what == ("+", "b", 4, 3):
                start(copy(cot_send, ct.at[z_lo], 2, one_r.at[2], partner), 2)
            continue
        if what[1] == "a":
            dist = what[2]
            a_arrives(dist)
            share([(dist, 0), (-dist, 0)] if dist < 4 else [(4, 0)])
        elif what[1] == "b":
            _, _, item, step = what
            b_arrives(item, step)
            share([(item, -step), (item, step)] if step < 4 else [(item, 4)])
        elif what[1] == "w":
            h = what[2]
            take(one_r.at[h])
            for way in range(2):
                y_send(way, 1, 1, h)
        else:
            kind, step, h = (0 if what[1] == "o" else 1), what[2], what[3]
            ways = [way for way in range(2) if step <= y_steps(way, kind)]
            take(y_sem(kind, step, h), len(ways))
            for way in ways:
                if step < y_steps(way, kind):
                    y_send(way, kind, step + 1, h)
        take_shared(False)

    def tokens_of(q, count):
        def stack(parts):
            return jnp.concatenate(parts, axis=0)

        return jnp.concatenate(
            [
                stack([tb[q + i, 0:64, :] for i in range(count)]),
                stack([tb[q + i, 64:128, :] for i in range(count)]),
                stack([tail[q + i, :, 0:96] for i in range(count)]),
            ],
            axis=1,
        )

    def forward(m, cc, acc):
        for j in range(4):
            w = jnp.concatenate([wb[cc, 4 * j + i] for i in range(4)], axis=1)
            acc += jnp.dot(w, tokens_of((m * 2 + cc) * 32 + 8 * j, 8), preferred_element_type=F32)
        return acc

    accs = [forward(m, core, jnp.zeros((ROWS, TOK), F32)) for m in range(2)]
    take_shared(True)
    accs = [forward(m, 1 - core, accs[m]) for m in range(2)]
    copy(cot_send, ct.at[1 - z_lo], 2, one_r.at[2], partner).wait_recv()
    for m in range(2):
        acc = accs[m]
        for t in range(3):
            wide = min(128, TOK - 128 * t)
            both[t, :, 0:wide] = acc[:, 128 * t : 128 * t + wide]
        for t in range(3):
            wide = min(128, TOK - 128 * t)
            gate = both[t, pl.ds(0, HALF, stride=2), :][:, 0:wide]
            up = both[t, pl.ds(1, HALF, stride=2), :][:, 0:wide]
            cot = ct[m, :, 128 * t : 128 * t + wide].astype(F32)[0:HALF]
            sig = jax.nn.sigmoid(gate)
            silu = gate * sig
            hid = jnp.concatenate([silu * up, jnp.zeros((8, wide), F32)], axis=0)
            hb[m, :, 128 * t : 128 * t + wide] = hid.astype(BF16)
            both[t, pl.ds(0, HALF, stride=2), 0:wide] = cot * up * sig * (1.0 + gate * (1.0 - sig))
            both[t, pl.ds(1, HALF, stride=2), 0:wide] = cot * silu
            dbt[m, :, 128 * t : 128 * t + wide] = both[t, :, 0:wide].astype(BF16)

    def partial(offset, kind, h):
        rows = row_block(kind, offset)
        total = jnp.zeros((ROWS, 128), F32)
        for m in range(2):
            total += lax.dot_general(
                dbt[m], tokens_of((m * 2 + h) * 32 + 2 * rows, 2), (((1,), (1,)), ((), ())), preferred_element_type=F32
            )
        return total

    order = {}
    for way in range(2):
        for kind in range(2):
            for step in range(1, y_steps(way, kind) + 1):
                for h in range(2):
                    order[way, kind, step, h] = len(order)

    def g_copy(way, kind, step, h):
        k = order[way, kind, step, h]
        return copy(rs_send.at[k], rs_recv.at[k], 1, g_r.at[k], on_y(1 - 2 * way))

    def arrived(way, kind, step, h):
        g_copy(way, kind, step, h).wait_recv()
        return rs_recv[order[way, kind, step, h]].astype(F32)

    def hop(way, kind, step, h):
        steps = y_steps(way, kind)
        total = partial((1 - 2 * way) * (steps + 1 - step), kind, h)
        if step > 1:
            total += arrived(way, kind, step - 1, h)
        rs_send[order[way, kind, step, h]] = total.astype(BF16)
        start(g_copy(way, kind, step, h), 1)

    up_order = [(kind, step, h) for step in range(1, 5) for kind in (0, 1) for h in (0, 1) if step <= y_steps(0, kind)]
    down_order = [(kind, step, h) for step in range(1, 3) for kind in (1, 0) for h in (0, 1)]
    down_order += [(1, 3, 0), (1, 3, 1), (0, 3, 0), (1, 4, 0), (1, 4, 1), (0, 3, 1)]
    for slot in range(14):
        hop(1, *down_order[slot])
        hop(0, *up_order[slot])
        if slot == 1:
            start(copy(hb.at[1 - z_lo], hid_recv, 3, one_r.at[3], partner), 3)
        if slot == 7:
            copy(hb.at[1 - z_lo], hid_recv, 3, one_r.at[3], partner).wait_recv()
            here = hb[z_lo].astype(F32)
            there = hid_recv[...].astype(F32)
            h_low = jnp.where(z_lo == 0, here, there)[0:HALF]
            h_high = jnp.where(z_lo == 0, there, here)[0 : HID - HALF]
            hid_keep[...] = jnp.concatenate([h_low, h_high], axis=0).astype(BF16)
            hid_copy = pltpu.make_async_copy(hid_keep, hid_out, out_sem.at[0])
            hid_copy.start()

    def fin_copy(h):
        return copy(fin_send.at[h], fin_recv.at[h], 1, one_r.at[4 + h], partner)

    for h in range(2):
        total = partial(0, 1, h)
        total += arrived(0, 1, 3, h)
        total += arrived(1, 1, 4, h)
        fin_send[h] = total.astype(BF16)
        start(fin_copy(h), 1)

    def put(parts, is_low):
        rows = jnp.concatenate(
            [parts[0][:, 0:64], parts[1][:, 0:64], parts[0][:, 64:128], parts[1][:, 64:128]], axis=1
        )

        rows = rows.reshape(HALF, 2, KB)

        @pl.when(is_low)
        def _():
            grad_out[0:HALF] = rows

        @pl.when(jnp.logical_not(is_low))
        def _():
            grad_out[HALF:HID] = rows[0 : HID - HALF]

    finals = []
    for h in range(2):
        total = partial(0, 0, h)
        total += arrived(1, 0, 3, h)
        total += arrived(0, 0, 4, h)
        finals.append(total)
    put(finals, z_lo == 0)
    for h in range(2):
        fin_copy(h).wait_recv()
    put([fin_recv[h].astype(F32) for h in range(2)], z_lo == 1)
    hid_copy.wait()
    for kind in range(2):
        all_left(kind)
    copy(cot_send, ct.at[z_lo], 2, one_r.at[2], partner).wait_send()
    copy(hb.at[1 - z_lo], hid_recv, 3, one_r.at[3], partner).wait_send()


def move(hid_in, grad_in, hid_out, grad_out, hid, grad, sem):
    arrive = [
        pltpu.make_async_copy(grad_in, grad, sem.at[0]),
        pltpu.make_async_copy(hid_in, hid, sem.at[1]),
    ]
    leave = [
        pltpu.make_async_copy(grad, grad_out, sem.at[2]),
        pltpu.make_async_copy(hid, hid_out, sem.at[3]),
    ]
    for c in arrive:
        c.start()
    for k in range(2):
        arrive[k].wait()
        leave[k].start()
    for c in leave:
        c.wait()


def body(tokens, codes, scales, cotangent):
    dma = pltpu.SemaphoreType.DMA
    vmem = pl.BlockSpec(memory_space=pltpu.VMEM)
    hbm = pl.BlockSpec(memory_space=pltpu.HBM)
    out_shape = (jax.ShapeDtypeStruct((HID, TOK), BF16), jax.ShapeDtypeStruct((HID, 2, KB), F32))
    results = pl.pallas_call(
        kernel,
        name="glu",
        out_shape=out_shape,
        in_specs=[hbm] * 4,
        out_specs=(hbm, vmem),
        scratch_shapes=[
            pltpu.VMEM((FEAT, TOK), BF16),
            pltpu.VMEM((2 * HALF, 2, KB), BF16),
            pltpu.VMEM((2, KB), BF16),
            pltpu.VMEM((HID, TOK), BF16),
            pltpu.VMEM((128, BLOCK, 128), BF16),
            pltpu.VMEM((128, FEAT, 128), BF16),
            pltpu.VMEM((2, 16, ROWS, 128), BF16),
            pltpu.VMEM((2, ROWS, 128), BF16),
            pltpu.VMEM((2, 96, TOK), BF16),
            pltpu.VMEM((96, TOK), BF16),
            pltpu.VMEM((2, 96, TOK), BF16),
            pltpu.VMEM((HID, TOK), BF16),
            pltpu.VMEM((96, TOK), BF16),
            pltpu.VMEM((3, ROWS, 128), F32),
            pltpu.VMEM((2, ROWS, TOK), BF16),
            pltpu.VMEM((28, ROWS, 128), BF16),
            pltpu.VMEM((28, ROWS, 128), BF16),
            pltpu.VMEM((2, ROWS, 128), BF16),
            pltpu.VMEM((2, ROWS, 128), BF16),
            dma((4,)), dma((1,)), dma((4,)), dma((4,)), dma((32,)), dma((19,)), dma((16,)), dma((6,)), dma((28,)),
        ],
        compiler_params=pltpu.CompilerParams(
            collective_id=0, has_side_effects=True, vmem_limit_bytes=56 * 2**20
        ),
    )(jnp.transpose(tokens), jnp.transpose(codes, (2, 1, 0)), jnp.transpose(scales), jnp.transpose(cotangent))
    hidden, grads = pl.pallas_call(
        move,
        name="move",
        out_shape=out_shape,
        in_specs=[hbm] * 2,
        out_specs=(hbm, hbm),
        scratch_shapes=[pltpu.VMEM((HID, TOK), BF16), pltpu.VMEM((HID, 2, KB), F32), dma((4,))],
        compiler_params=pltpu.CompilerParams(vmem_limit_bytes=56 * 2**20),
    )(*results)
    return jnp.transpose(hidden), jnp.transpose(grads, (2, 1, 0))


def solution(mesh):
    in_specs = (P("local", "node"), P("local", None, "node"), P("local", None), P("local", "node"))
    out_specs = (P("local", "node"), P("local", None, "node"))
    return jax.shard_map(body, mesh=mesh, in_specs=in_specs, out_specs=out_specs, check_vma=False)
```

```python
import jax
import jax.numpy as jnp
from jax import lax
from jax.experimental import pallas as pl
from jax.experimental.pallas import tpu as pltpu
from jax.sharding import PartitionSpec as P

MESH = pl.DeviceIdType.MESH
F32 = jnp.float32
BF16 = jnp.bfloat16
TOK = 352
FEAT = 64
HID = 172
HALF = 88
ROWS = 2 * HALF
KB = 256
RING = 8
BLOCK = 176
CUT = 96

FIRST = [
    ("+", "a", 2), ("+", "a", 1), ("+", "b", 0, 1),
]
STEPS = [
    ("-", "a", 2), ("+", "a", 3), ("+", "a", 4), ("+", "b", 2, 1), ("-", "a", 1), ("+", "b", -2, 1), ("+", "b", 1, 1),
    ("+", "b", -1, 1), ("-", "b", 0, 1), ("-", "w", 0), ("+", "b", 0, 2), ("-", "w", 1), ("-", "o", 1, 0),
    ("-", "a", 3), ("+", "b", 3, 1), ("+", "b", -3, 1), ("-", "o", 1, 1), ("-", "a", 4), ("+", "b", 4, 1),
    ("-", "b", 2, 1), ("+", "b", 2, 2), ("-", "b", -2, 1), ("+", "b", -2, 2), ("-", "b", 1, 1), ("+", "b", 1, 2),
    ("-", "p", 1, 0), ("-", "b", -1, 1), ("+", "b", -1, 2), ("-", "b", 0, 2), ("+", "b", 0, 3), ("-", "p", 1, 1),
    ("-", "b", 3, 1), ("+", "b", 3, 2), ("-", "b", -3, 1), ("+", "b", -3, 2), ("-", "o", 2, 0), ("-", "b", 4, 1),
    ("+", "b", 4, 2), ("-", "b", 2, 2), ("+", "b", 2, 3), ("-", "o", 2, 1), ("-", "b", -2, 2), ("+", "b", -2, 3),
    ("-", "b", 1, 2), ("+", "b", 1, 3), ("-", "p", 2, 0), ("-", "b", -1, 2), ("+", "b", -1, 3), ("-", "b", 0, 3),
    ("+", "b", 0, 4), ("-", "p", 2, 1), ("-", "b", 3, 2), ("+", "b", 3, 3), ("-", "b", -3, 2), ("+", "b", -3, 3),
    ("-", "o", 3, 0), ("-", "b", 4, 2), ("+", "b", 4, 4), ("+", "b", 4, 3), ("-", "b", 2, 3), ("-", "o", 3, 1),
    ("+", "b", 2, 4), ("-", "b", -2, 3), ("+", "b", -2, 4), ("-", "b", 1, 3), ("+", "b", 1, 4), ("-", "p", 3, 0),
    ("-", "b", -1, 3), ("+", "b", -1, 4), ("-", "b", 0, 4), ("-", "b", 3, 3), ("+", "b", 3, 4), ("-", "p", 3, 1),
    ("-", "b", -3, 3), ("+", "b", -3, 4), ("-", "o", 4, 0), ("-", "b", 4, 4), ("-", "b", 4, 3), ("-", "b", 2, 4),
    ("-", "b", -2, 4), ("-", "o", 4, 1), ("-", "b", 1, 4), ("-", "p", 4, 0), ("-", "b", -1, 4), ("-", "b", 3, 4),
    ("-", "b", -3, 4), ("-", "p", 4, 1),
]


def kernel(
    tok_hbm, codes_hbm, scales_hbm, cot_hbm, hid_out, grad_out,
    tok, codes, scales, cots, tb, tail, wb, w_other, ct, cot_send, hb, hid_keep, hid_recv, both, dbt, grad, rs_send, rs_recv,
    fin_send, fin_recv, in_sem, out_sem, sent_sem, a_r, b_r, sib_r, y_r, one_r, g_r,
):
    loads = [
        pltpu.make_async_copy(tok_hbm, tok, in_sem.at[0]),
        pltpu.make_async_copy(codes_hbm, codes.at[pl.ds(0, HID)], in_sem.at[1]),
        pltpu.make_async_copy(scales_hbm, scales, in_sem.at[2]),
        pltpu.make_async_copy(cot_hbm, cots, in_sem.at[3]),
    ]
    for c in loads:
        c.start()

    node, local = lax.axis_index("node"), lax.axis_index("local")
    core = lax.rem(node, 2)
    x = lax.rem(lax.div(node, 2), 8)
    z_lo = lax.rem(local, 2)
    z = lax.div(node, 16) * 2 + z_lo
    y = lax.div(local, 2)

    def wrap(v):
        return lax.rem(v + RING, RING)

    def device(cx, cy, cz, cc):
        return (lax.div(cz, 2) * 16 + cx * 2 + cc, cy * 2 + lax.rem(cz, 2))

    first, second = jnp.where(core == 0, x, z), jnp.where(core == 0, z, x)

    def at(a, b):
        return jnp.where(core == 0, a, b), jnp.where(core == 0, b, a)

    def on_first(step):
        cx, cz = at(wrap(first + step), second)
        return device(cx, y, cz, core)

    def on_second(step):
        cx, cz = at(first, wrap(second + step))
        return device(cx, y, cz, core)

    def on_y(step):
        return device(x, wrap(y + step), z, core)

    sibling = device(x, y, z, 1 - core)
    other_z = lax.div(z, 2) * 2 + (1 - z_lo)
    partner = device(x, y, other_z, core)

    def on_y_partner(step):
        return device(x, wrap(y + step), other_z, core)

    def block_index(cx, cz, cc):
        return (lax.rem(cz, 2) * 2 + cc) * 32 + lax.div(cz, 2) * 8 + cx

    first_at = {a: wrap(first + a) for a in range(-4, 5)}
    second_at = {b: wrap(second + b) for b in range(-4, 5)}

    def index_of(a, b):
        cx, cz = at(first_at[a], second_at[b])
        return block_index(cx, cz, core)

    def sibling_index(a, b):
        cx, cz = at(first_at[b], second_at[a])
        return block_index(cx, cz, 1 - core)

    def block(index, part=None):
        if part is None:
            return tb.at[index]
        return tb.at[index, pl.ds(0, CUT) if part == 0 else pl.ds(CUT, BLOCK - CUT), :]

    pieces = [0, 0]

    def copy(src, dst, kind, recv_sem, target):
        return pltpu.make_async_remote_copy(
            src_ref=src, dst_ref=dst, send_sem=sent_sem.at[kind], recv_sem=recv_sem, device_id=target,
            device_id_type=MESH,
        )

    def start(c, kind, count=1):
        c.start()
        if kind < 2:
            pieces[kind] += count

    def take(recv_sem, count=1):
        ref = tb.at[pl.ds(0, count)]
        copy(ref, ref, 0, recv_sem, sibling).wait_recv()

    def all_left(kind):
        ref = tb.at[pl.ds(0, round(pieces[kind]))]
        copy(ref, ref, kind, a_r.at[0], sibling).wait_send()

    barrier = pltpu.get_barrier_semaphore()
    peers = [sibling, on_y(1), on_y(-1), on_y_partner(1), on_y_partner(-1)]
    for step in (1, -1, 2, -2):
        peers += [on_first(step), on_second(step)]
    for peer in peers:
        pl.semaphore_signal(barrier, inc=1, device_id=peer, device_id_type=MESH)

    own = index_of(0, 0)
    loads[0].wait()
    t = tok[...]
    tb[own, 0:64, :] = t[:, 0:128]
    tb[own, 64:128, :] = t[:, 128:256]
    rest = t[:, 256:352]
    tail[own, :, 0:96] = rest
    r = [rest[16 * i : 16 * i + 16, :] for i in range(4)]
    tb[own, 128:144, :] = jnp.concatenate([r[0], r[1][:, 0:32]], axis=1)
    tb[own, 144:160, :] = jnp.concatenate([r[1][:, 32:96], r[2][:, 0:64]], axis=1)
    tb[own, 160:176, :] = jnp.concatenate([r[2][:, 64:96], r[3]], axis=1)

    codes[HID : 2 * HALF] = jnp.zeros((2 * HALF - HID, 2, KB), BF16)
    loads[1].wait()
    loads[2].wait()
    scale = scales[...].astype(F32)[None]

    def weights(half):
        part = codes[pl.ds(half * HALF, HALF)].astype(F32) * scale
        w = part.reshape(ROWS, KB).astype(BF16)
        return (
            jnp.concatenate([w[:, 0:64], w[:, 128:192]], axis=1),
            jnp.concatenate([w[:, 64:128], w[:, 192:256]], axis=1),
        )

    for h, w in enumerate(weights(1 - z_lo)):
        w_other[h] = w
    pl.semaphore_wait(barrier, len(peers))

    def unpack(q):
        p0, p1, p2 = tb[q, 128:144, :], tb[q, 144:160, :], tb[q, 160:176, :]
        tail[q, 0:16, 0:96] = p0[:, 0:96]
        tail[q, 16:32, 0:96] = jnp.concatenate([p0[:, 96:128], p1[:, 0:64]], axis=1)
        tail[q, 32:48, 0:96] = jnp.concatenate([p1[:, 64:128], p2[:, 0:32]], axis=1)
        tail[q, 48:64, 0:96] = p2[:, 32:128]

    def a_send(way, dist):
        sign = 1 - 2 * way
        if dist <= 2:
            at_a, hops, part = 0, dist, None
        elif dist == 3:
            at_a, hops, part = -2 * sign, 1, None
        else:
            at_a, hops, part = -2 * sign, 2, way
        ref = block(index_of(at_a, 0), part)
        start(copy(ref, ref, 0, a_r.at[dist - 1], on_first(sign * hops)), 0, share_of(dist, way))

    def share_of(step, way):
        return 1 if step < 4 else (CUT if way == 0 else BLOCK - CUT) / BLOCK

    def a_arrives(dist):
        take(a_r.at[dist - 1], 2 if dist < 4 else 1)

    def b_sem(item, step):
        return b_r.at[(item + 3) * 4 + step - 1]

    def b_send(way, item, step):
        sign = 1 - 2 * way
        hops = 2 if (item, step) == (4, 4) else 1
        ref = block(index_of(item, -sign * (step - hops)), way if step == 4 else None)
        start(copy(ref, ref, 0, b_sem(item, step), on_second(sign * hops)), 0, share_of(step, way))

    def b_arrives(item, step):
        take(b_sem(item, step), 2 if step < 4 else 1)

    shared = [[]]
    taken = [0]

    def share(blocks):
        if len(shared[-1]) == 4 or len(shared) == 1 and shared[0] == [(0, 0)]:
            shared.append([])
        for a, b in blocks:
            q = index_of(a, b)
            start(copy(block(q), block(q), 0, sib_r.at[len(shared) - 1], sibling), 0)
            shared[-1].append((a, b))
            if (a, b) != (0, 0):
                unpack(q)

    def take_shared(all_of_them):
        while taken[0] < len(shared) - (0 if all_of_them else 2):
            group = shared[taken[0]]
            take(sib_r.at[taken[0]], len(group))
            for a, b in group:
                unpack(sibling_index(a, b))
            taken[0] += 1

    def y_sem(kind, step, h):
        return y_r.at[(kind * 4 + step - 1) * 2 + h]

    def row_block(kind, offset):
        return 2 * wrap(y + offset) + (z_lo if kind == 0 else 1 - z_lo)

    def y_steps(way, kind):
        return 4 if way == kind else 3

    def y_send(way, kind, step, h):
        sign = 1 - 2 * way
        ref = wb.at[h, row_block(kind, -sign * (step - 1))]
        start(copy(ref, ref, 1, y_sem(kind, step, h), on_y(sign)), 1)

    mine = row_block(0, 0)
    theirs = row_block(1, 0)

    def w_copy(h, dst):
        return copy(w_other.at[h], wb.at[h, dst], 1, one_r.at[h], partner)

    def token_send(what):
        for way in range(2):
            if what[1] == "a":
                a_send(way, what[2])
            else:
                b_send(way, what[2], what[3])

    for what in FIRST:
        token_send(what)
    share([(0, 0)])

    for h in range(2):
        start(w_copy(h, mine), 1)
    for h, w in enumerate(weights(z_lo)):
        wb[h, mine] = w
        for way in range(2):
            y_send(way, 0, 1, h)

    loads[3].wait()
    cot = cots[...].astype(F32)
    low, high = cot[0:HALF], jnp.concatenate([cot[HALF:HID], jnp.zeros((2 * HALF - HID, TOK), F32)], axis=0)
    pad = jnp.zeros((8, TOK), F32)
    ct[z_lo] = jnp.concatenate([jnp.where(z_lo == 0, low, high), pad], axis=0).astype(BF16)
    cot_send[...] = jnp.concatenate([jnp.where(z_lo == 0, high, low), pad], axis=0).astype(BF16)

    for what in STEPS:
        if what[0] == "+":
            token_send(what)
            if what == ("+", "b", 4, 3):
                start(copy(cot_send, ct.at[z_lo], 2, one_r.at[2], partner), 2)
            continue
        if what[1] == "a":
            dist = what[2]
            a_arrives(dist)
            share([(dist, 0), (-dist, 0)] if dist < 4 else [(4, 0)])
        elif what[1] == "b":
            _, _, item, step = what
            b_arrives(item, step)
            share([(item, -step), (item, step)] if step < 4 else [(item, 4)])
        elif what[1] == "w":
            h = what[2]
            take(one_r.at[h])
            for way in range(2):
                y_send(way, 1, 1, h)
        else:
            kind, step, h = (0 if what[1] == "o" else 1), what[2], what[3]
            ways = [way for way in range(2) if step <= y_steps(way, kind)]
            take(y_sem(kind, step, h), len(ways))
            for way in ways:
                if step < y_steps(way, kind):
                    y_send(way, kind, step + 1, h)
        take_shared(False)

    def tokens_of(q, count):
        def stack(parts):
            return jnp.concatenate(parts, axis=0)

        return jnp.concatenate(
            [
                stack([tb[q + i, 0:64, :] for i in range(count)]),
                stack([tb[q + i, 64:128, :] for i in range(count)]),
                stack([tail[q + i, :, 0:96] for i in range(count)]),
            ],
            axis=1,
        )

    def forward(m, cc, acc):
        for j in range(4):
            w = jnp.concatenate([wb[cc, 4 * j + i] for i in range(4)], axis=1)
            acc += jnp.dot(w, tokens_of((m * 2 + cc) * 32 + 8 * j, 8), preferred_element_type=F32)
        return acc

    accs = [forward(m, core, jnp.zeros((ROWS, TOK), F32)) for m in range(2)]
    take_shared(True)
    accs = [forward(m, 1 - core, accs[m]) for m in range(2)]
    copy(cot_send, ct.at[1 - z_lo], 2, one_r.at[2], partner).wait_recv()
    for m in range(2):
        acc = accs[m]
        for t in range(3):
            wide = min(128, TOK - 128 * t)
            both[t, :, 0:wide] = acc[:, 128 * t : 128 * t + wide]
        for t in range(3):
            wide = min(128, TOK - 128 * t)
            gate = both[t, pl.ds(0, HALF, stride=2), :][:, 0:wide]
            up = both[t, pl.ds(1, HALF, stride=2), :][:, 0:wide]
            cot = ct[m, :, 128 * t : 128 * t + wide].astype(F32)[0:HALF]
            sig = jax.nn.sigmoid(gate)
            silu = gate * sig
            hid = jnp.concatenate([silu * up, jnp.zeros((8, wide), F32)], axis=0)
            hb[m, :, 128 * t : 128 * t + wide] = hid.astype(BF16)
            both[t, pl.ds(0, HALF, stride=2), 0:wide] = cot * up * sig * (1.0 + gate * (1.0 - sig))
            both[t, pl.ds(1, HALF, stride=2), 0:wide] = cot * silu
            dbt[m, :, 128 * t : 128 * t + wide] = both[t, :, 0:wide].astype(BF16)

    def partial(offset, kind, h):
        rows = row_block(kind, offset)
        total = jnp.zeros((ROWS, 128), F32)
        for m in range(2):
            total += lax.dot_general(
                dbt[m], tokens_of((m * 2 + h) * 32 + 2 * rows, 2), (((1,), (1,)), ((), ())), preferred_element_type=F32
            )
        return total

    order = {}
    for way in range(2):
        for kind in range(2):
            for step in range(1, y_steps(way, kind) + 1):
                for h in range(2):
                    order[way, kind, step, h] = len(order)

    def g_copy(way, kind, step, h):
        k = order[way, kind, step, h]
        to = on_y_partner if kind == 1 and step == y_steps(way, kind) else on_y
        return copy(rs_send.at[k], rs_recv.at[k], 1, g_r.at[k], to(1 - 2 * way))

    def arrived(way, kind, step, h):
        g_copy(way, kind, step, h).wait_recv()
        return rs_recv[order[way, kind, step, h]].astype(F32)

    def hop(way, kind, step, h):
        steps = y_steps(way, kind)
        total = partial((1 - 2 * way) * (steps + 1 - step), kind, h)
        if step > 1:
            total += arrived(way, kind, step - 1, h)
        rs_send[order[way, kind, step, h]] = total.astype(BF16)
        start(g_copy(way, kind, step, h), 1)

    def fin_copy(h):
        return copy(fin_send.at[h], fin_recv.at[h], 1, one_r.at[4 + h], partner)

    up_order = [(kind, step, h) for step in range(1, 5) for kind in (0, 1) for h in (0, 1) if step <= y_steps(0, kind)]
    down_order = [(kind, step, h) for step in range(1, 3) for kind in (1, 0) for h in (0, 1)]
    down_order += [(1, 3, 0), (1, 3, 1), (0, 3, 0), (1, 4, 0), (1, 4, 1), (0, 3, 1)]
    for slot in range(14):
        hop(1, *down_order[slot])
        hop(0, *up_order[slot])
        if slot == 1:
            start(copy(hb.at[1 - z_lo], hid_recv, 3, one_r.at[3], partner), 3)
        if slot in (4, 5):
            fin_send[slot - 4] = partial(0, 1, slot - 4).astype(BF16)
            start(fin_copy(slot - 4), 1)
        if slot == 7:
            copy(hb.at[1 - z_lo], hid_recv, 3, one_r.at[3], partner).wait_recv()
            here = hb[z_lo].astype(F32)
            there = hid_recv[...].astype(F32)
            h_low = jnp.where(z_lo == 0, here, there)[0:HALF]
            h_high = jnp.where(z_lo == 0, there, here)[0 : HID - HALF]
            hid_keep[...] = jnp.concatenate([h_low, h_high], axis=0).astype(BF16)
            hid_copy = pltpu.make_async_copy(hid_keep, hid_out, out_sem.at[0])
            hid_copy.start()

    def put(parts, is_low):
        rows = jnp.concatenate(
            [parts[0][:, 0:64], parts[1][:, 0:64], parts[0][:, 64:128], parts[1][:, 64:128]], axis=1
        )

        rows = rows.reshape(HALF, 2, KB)

        @pl.when(is_low)
        def _():
            grad[0:HALF] = rows
            grad_copies[0].start()

        @pl.when(jnp.logical_not(is_low))
        def _():
            grad[HALF:HID] = rows[0 : HID - HALF]
            grad_copies[1].start()

    grad_copies = [
        pltpu.make_async_copy(grad.at[pl.ds(lo, n)], grad_out.at[pl.ds(lo, n)], out_sem.at[k])
        for k, lo, n in ((1, 0, HALF), (2, HALF, HID - HALF))
    ]
    own_terms = [partial(0, 0, h) for h in range(2)]
    others = []
    for h in range(2):
        fin_copy(h).wait_recv()
        others.append(fin_recv[h].astype(F32) + arrived(0, 1, 3, h) + arrived(1, 1, 4, h))
    put(others, z_lo == 1)
    put([own_terms[h] + arrived(1, 0, 3, h) + arrived(0, 0, 4, h) for h in range(2)], z_lo == 0)
    for c in grad_copies:
        c.wait()
    hid_copy.wait()
    for kind in range(2):
        all_left(kind)
    copy(cot_send, ct.at[z_lo], 2, one_r.at[2], partner).wait_send()
    copy(hb.at[1 - z_lo], hid_recv, 3, one_r.at[3], partner).wait_send()


def move(hid_in, grad_in, hid_out, grad_out, hid, grad, sem):
    arrive = [
        pltpu.make_async_copy(grad_in, grad, sem.at[0]),
        pltpu.make_async_copy(hid_in, hid, sem.at[1]),
    ]
    leave = [
        pltpu.make_async_copy(grad, grad_out, sem.at[2]),
        pltpu.make_async_copy(hid, hid_out, sem.at[3]),
    ]
    for c in arrive:
        c.start()
    for k in range(2):
        arrive[k].wait()
        leave[k].start()
    for c in leave:
        c.wait()


def body(tokens, codes, scales, cotangent):
    dma = pltpu.SemaphoreType.DMA
    hbm = pl.BlockSpec(memory_space=pltpu.HBM)
    out_shape = (jax.ShapeDtypeStruct((HID, TOK), BF16), jax.ShapeDtypeStruct((HID, 2, KB), F32))
    results = pl.pallas_call(
        kernel,
        name="glu",
        out_shape=out_shape,
        in_specs=[hbm] * 4,
        out_specs=(hbm, hbm),
        scratch_shapes=[
            pltpu.VMEM((FEAT, TOK), BF16),
            pltpu.VMEM((2 * HALF, 2, KB), BF16),
            pltpu.VMEM((2, KB), BF16),
            pltpu.VMEM((HID, TOK), BF16),
            pltpu.VMEM((128, BLOCK, 128), BF16),
            pltpu.VMEM((128, FEAT, 128), BF16),
            pltpu.VMEM((2, 16, ROWS, 128), BF16),
            pltpu.VMEM((2, ROWS, 128), BF16),
            pltpu.VMEM((2, 96, TOK), BF16),
            pltpu.VMEM((96, TOK), BF16),
            pltpu.VMEM((2, 96, TOK), BF16),
            pltpu.VMEM((HID, TOK), BF16),
            pltpu.VMEM((96, TOK), BF16),
            pltpu.VMEM((3, ROWS, 128), F32),
            pltpu.VMEM((2, ROWS, TOK), BF16),
            pltpu.VMEM((HID, 2, KB), F32),
            pltpu.VMEM((28, ROWS, 128), BF16),
            pltpu.VMEM((28, ROWS, 128), BF16),
            pltpu.VMEM((2, ROWS, 128), BF16),
            pltpu.VMEM((2, ROWS, 128), BF16),
            dma((4,)), dma((3,)), dma((4,)), dma((4,)), dma((32,)), dma((19,)), dma((16,)), dma((6,)), dma((28,)),
        ],
        compiler_params=pltpu.CompilerParams(
            collective_id=0, has_side_effects=True, vmem_limit_bytes=56 * 2**20
        ),
    )(jnp.transpose(tokens), jnp.transpose(codes, (2, 1, 0)), jnp.transpose(scales), jnp.transpose(cotangent))
    hidden, grads = pl.pallas_call(
        move,
        name="move",
        out_shape=out_shape,
        in_specs=[hbm] * 2,
        out_specs=(hbm, hbm),
        scratch_shapes=[pltpu.VMEM((HID, TOK), BF16), pltpu.VMEM((HID, 2, KB), F32), dma((4,))],
        compiler_params=pltpu.CompilerParams(vmem_limit_bytes=56 * 2**20),
    )(*results)
    return jnp.transpose(hidden), jnp.transpose(grads, (2, 1, 0))


def solution(mesh):
    in_specs = (P("local", "node"), P("local", None, "node"), P("local", None), P("local", "node"))
    out_specs = (P("local", "node"), P("local", None, "node"))
    return jax.shard_map(body, mesh=mesh, in_specs=in_specs, out_specs=out_specs, check_vma=False)
```

```python
import jax
import jax.numpy as jnp
from jax import lax
from jax.experimental import pallas as pl
from jax.experimental.pallas import tpu as pltpu
from jax.sharding import PartitionSpec as P

MESH = pl.DeviceIdType.MESH
F32 = jnp.float32
BF16 = jnp.bfloat16
TOK = 352
FEAT = 64
HID = 172
HALF = 88
ROWS = 2 * HALF
KB = 256
RING = 8
BLOCK = 176
CUT = 96

FIRST = [
    ("+", "a", 2), ("+", "a", 1), ("+", "b", 0, 1),
]
STEPS = [
    ("-", "a", 2), ("+", "a", 3), ("+", "a", 4), ("+", "b", 2, 1), ("-", "a", 1), ("+", "b", -2, 1), ("+", "b", 1, 1),
    ("+", "b", -1, 1), ("-", "b", 0, 1), ("-", "w", 0), ("+", "b", 0, 2), ("-", "w", 1), ("-", "o", 1, 0),
    ("-", "a", 3), ("+", "b", 3, 1), ("+", "b", -3, 1), ("-", "o", 1, 1), ("-", "a", 4), ("+", "b", 4, 1),
    ("-", "b", 2, 1), ("+", "b", 2, 2), ("-", "b", -2, 1), ("+", "b", -2, 2), ("-", "b", 1, 1), ("+", "b", 1, 2),
    ("-", "p", 1, 0), ("-", "b", -1, 1), ("+", "b", -1, 2), ("-", "b", 0, 2), ("+", "b", 0, 3), ("-", "p", 1, 1),
    ("-", "b", 3, 1), ("+", "b", 3, 2), ("-", "b", -3, 1), ("+", "b", -3, 2), ("-", "o", 2, 0), ("-", "b", 4, 1),
    ("+", "b", 4, 2), ("-", "b", 2, 2), ("+", "b", 2, 3), ("-", "o", 2, 1), ("-", "b", -2, 2), ("+", "b", -2, 3),
    ("-", "b", 1, 2), ("+", "b", 1, 3), ("-", "p", 2, 0), ("-", "b", -1, 2), ("+", "b", -1, 3), ("-", "b", 0, 3),
    ("+", "b", 0, 4), ("-", "p", 2, 1), ("-", "b", 3, 2), ("+", "b", 3, 3), ("-", "b", -3, 2), ("+", "b", -3, 3),
    ("-", "o", 3, 0), ("-", "b", 4, 2), ("+", "b", 4, 4), ("+", "b", 4, 3), ("-", "b", 2, 3), ("-", "o", 3, 1),
    ("+", "b", 2, 4), ("-", "b", -2, 3), ("+", "b", -2, 4), ("-", "b", 1, 3), ("+", "b", 1, 4), ("-", "p", 3, 0),
    ("-", "b", -1, 3), ("+", "b", -1, 4), ("-", "b", 0, 4), ("-", "b", 3, 3), ("+", "b", 3, 4), ("-", "p", 3, 1),
    ("-", "b", -3, 3), ("+", "b", -3, 4), ("-", "o", 4, 0), ("-", "b", 4, 4), ("-", "b", 4, 3), ("-", "b", 2, 4),
    ("-", "b", -2, 4), ("-", "o", 4, 1), ("-", "b", 1, 4), ("-", "p", 4, 0), ("-", "b", -1, 4), ("-", "b", 3, 4),
    ("-", "b", -3, 4), ("-", "p", 4, 1),
]


def kernel(
    tok_hbm, codes_hbm, scales_hbm, cot_hbm, hid_out, grad_out,
    tok, codes, scales, cots, tb, tail, wb, w_other, ct, cot_send, hb, hid_keep, hid_recv, both, dbt, grad, rs_send, rs_recv,
    fin_send, fin_recv, in_sem, out_sem, sent_sem, a_r, b_r, sib_r, y_r, one_r, g_r,
):
    loads = [
        pltpu.make_async_copy(tok_hbm, tok, in_sem.at[0]),
        pltpu.make_async_copy(codes_hbm, codes.at[pl.ds(0, HID)], in_sem.at[1]),
        pltpu.make_async_copy(scales_hbm, scales, in_sem.at[2]),
        pltpu.make_async_copy(cot_hbm, cots, in_sem.at[3]),
    ]
    for c in loads:
        c.start()

    node, local = lax.axis_index("node"), lax.axis_index("local")
    core = lax.rem(node, 2)
    x = lax.rem(lax.div(node, 2), 8)
    z_lo = lax.rem(local, 2)
    z = lax.div(node, 16) * 2 + z_lo
    y = lax.div(local, 2)

    def wrap(v):
        return lax.rem(v + RING, RING)

    def device(cx, cy, cz, cc):
        return (lax.div(cz, 2) * 16 + cx * 2 + cc, cy * 2 + lax.rem(cz, 2))

    first, second = jnp.where(core == 0, x, z), jnp.where(core == 0, z, x)

    def at(a, b):
        return jnp.where(core == 0, a, b), jnp.where(core == 0, b, a)

    def on_first(step):
        cx, cz = at(wrap(first + step), second)
        return device(cx, y, cz, core)

    def on_second(step):
        cx, cz = at(first, wrap(second + step))
        return device(cx, y, cz, core)

    def on_y(step):
        return device(x, wrap(y + step), z, core)

    sibling = device(x, y, z, 1 - core)
    other_z = lax.div(z, 2) * 2 + (1 - z_lo)
    partner = device(x, y, other_z, core)

    def on_y_partner(step):
        return device(x, wrap(y + step), other_z, core)

    def block_index(cx, cz, cc):
        return (lax.rem(cz, 2) * 2 + cc) * 32 + lax.div(cz, 2) * 8 + cx

    first_at = {a: wrap(first + a) for a in range(-4, 5)}
    second_at = {b: wrap(second + b) for b in range(-4, 5)}

    def index_of(a, b):
        cx, cz = at(first_at[a], second_at[b])
        return block_index(cx, cz, core)

    def sibling_index(a, b):
        cx, cz = at(first_at[b], second_at[a])
        return block_index(cx, cz, 1 - core)

    def block(index, part=None):
        if part is None:
            return tb.at[index]
        return tb.at[index, pl.ds(0, CUT) if part == 0 else pl.ds(CUT, BLOCK - CUT), :]

    pieces = [0, 0]

    def copy(src, dst, kind, recv_sem, target):
        return pltpu.make_async_remote_copy(
            src_ref=src, dst_ref=dst, send_sem=sent_sem.at[kind], recv_sem=recv_sem, device_id=target,
            device_id_type=MESH,
        )

    def start(c, kind, count=1):
        c.start()
        if kind < 2:
            pieces[kind] += count

    def take(recv_sem, count=1):
        ref = tb.at[pl.ds(0, count)]
        copy(ref, ref, 0, recv_sem, sibling).wait_recv()

    def all_left(kind):
        ref = tb.at[pl.ds(0, round(pieces[kind]))]
        copy(ref, ref, kind, a_r.at[0], sibling).wait_send()

    barrier = pltpu.get_barrier_semaphore()
    peers = [sibling, on_y(1), on_y(-1), on_y_partner(1), on_y_partner(-1)]
    for step in (1, -1, 2, -2):
        peers += [on_first(step), on_second(step)]
    for peer in peers:
        pl.semaphore_signal(barrier, inc=1, device_id=peer, device_id_type=MESH)

    own = index_of(0, 0)
    loads[0].wait()
    t = tok[...]
    tb[own, 0:64, :] = t[:, 0:128]
    tb[own, 64:128, :] = t[:, 128:256]
    rest = t[:, 256:352]
    tail[own, :, 0:96] = rest
    r = [rest[16 * i : 16 * i + 16, :] for i in range(4)]
    tb[own, 128:144, :] = jnp.concatenate([r[0], r[1][:, 0:32]], axis=1)
    tb[own, 144:160, :] = jnp.concatenate([r[1][:, 32:96], r[2][:, 0:64]], axis=1)
    tb[own, 160:176, :] = jnp.concatenate([r[2][:, 64:96], r[3]], axis=1)

    codes[HID : 2 * HALF] = jnp.zeros((2 * HALF - HID, 2, KB), BF16)
    loads[1].wait()
    loads[2].wait()
    scale = scales[...].astype(F32)[None]

    def weights(half):
        part = codes[pl.ds(half * HALF, HALF)].astype(F32) * scale
        w = part.reshape(ROWS, KB).astype(BF16)
        return (
            jnp.concatenate([w[:, 0:64], w[:, 128:192]], axis=1),
            jnp.concatenate([w[:, 64:128], w[:, 192:256]], axis=1),
        )

    for h, w in enumerate(weights(1 - z_lo)):
        w_other[h] = w
    pl.semaphore_wait(barrier, len(peers))

    def unpack(q):
        p0, p1, p2 = tb[q, 128:144, :], tb[q, 144:160, :], tb[q, 160:176, :]
        tail[q, 0:16, 0:96] = p0[:, 0:96]
        tail[q, 16:32, 0:96] = jnp.concatenate([p0[:, 96:128], p1[:, 0:64]], axis=1)
        tail[q, 32:48, 0:96] = jnp.concatenate([p1[:, 64:128], p2[:, 0:32]], axis=1)
        tail[q, 48:64, 0:96] = p2[:, 32:128]

    def a_send(way, dist):
        sign = 1 - 2 * way
        if dist <= 2:
            at_a, hops, part = 0, dist, None
        elif dist == 3:
            at_a, hops, part = -2 * sign, 1, None
        else:
            at_a, hops, part = -2 * sign, 2, way
        ref = block(index_of(at_a, 0), part)
        start(copy(ref, ref, 0, a_r.at[dist - 1], on_first(sign * hops)), 0, share_of(dist, way))

    def share_of(step, way):
        return 1 if step < 4 else (CUT if way == 0 else BLOCK - CUT) / BLOCK

    def a_arrives(dist):
        take(a_r.at[dist - 1], 2 if dist < 4 else 1)

    def b_sem(item, step):
        return b_r.at[(item + 3) * 4 + step - 1]

    def b_send(way, item, step):
        sign = 1 - 2 * way
        hops = 2 if (item, step) == (4, 4) else 1
        ref = block(index_of(item, -sign * (step - hops)), way if step == 4 else None)
        start(copy(ref, ref, 0, b_sem(item, step), on_second(sign * hops)), 0, share_of(step, way))

    def b_arrives(item, step):
        take(b_sem(item, step), 2 if step < 4 else 1)

    shared = [[]]
    taken = [0]

    def share(blocks):
        if len(shared[-1]) == 4 or len(shared) == 1 and shared[0] == [(0, 0)]:
            shared.append([])
        for a, b in blocks:
            q = index_of(a, b)
            start(copy(block(q), block(q), 0, sib_r.at[len(shared) - 1], sibling), 0)
            shared[-1].append((a, b))
            if (a, b) != (0, 0):
                unpack(q)

    def take_shared(all_of_them):
        while taken[0] < len(shared) - (0 if all_of_them else 2):
            group = shared[taken[0]]
            take(sib_r.at[taken[0]], len(group))
            for a, b in group:
                unpack(sibling_index(a, b))
            taken[0] += 1

    def y_sem(kind, step, h):
        return y_r.at[(kind * 4 + step - 1) * 2 + h]

    def row_block(kind, offset):
        return 2 * wrap(y + offset) + (z_lo if kind == 0 else 1 - z_lo)

    def y_steps(way, kind):
        return 4 if way == kind else 3

    def y_send(way, kind, step, h):
        sign = 1 - 2 * way
        ref = wb.at[h, row_block(kind, -sign * (step - 1))]
        start(copy(ref, ref, 1, y_sem(kind, step, h), on_y(sign)), 1)

    mine = row_block(0, 0)
    theirs = row_block(1, 0)

    def w_copy(h, dst):
        return copy(w_other.at[h], wb.at[h, dst], 1, one_r.at[h], partner)

    def token_send(what):
        for way in range(2):
            if what[1] == "a":
                a_send(way, what[2])
            else:
                b_send(way, what[2], what[3])

    for what in FIRST:
        token_send(what)
    share([(0, 0)])

    for h in range(2):
        start(w_copy(h, mine), 1)
    for h, w in enumerate(weights(z_lo)):
        wb[h, mine] = w
        for way in range(2):
            y_send(way, 0, 1, h)

    loads[3].wait()
    cot = cots[...].astype(F32)
    low, high = cot[0:HALF], jnp.concatenate([cot[HALF:HID], jnp.zeros((2 * HALF - HID, TOK), F32)], axis=0)
    pad = jnp.zeros((8, TOK), F32)
    ct[z_lo] = jnp.concatenate([jnp.where(z_lo == 0, low, high), pad], axis=0).astype(BF16)
    cot_send[...] = jnp.concatenate([jnp.where(z_lo == 0, high, low), pad], axis=0).astype(BF16)

    last_send = [what for what in STEPS if what[0] == "+"][-1]
    for what in STEPS:
        if what[0] == "+":
            token_send(what)
            if what == last_send:
                start(copy(cot_send, ct.at[z_lo], 2, one_r.at[2], partner), 2)
            continue
        if what[1] == "a":
            dist = what[2]
            a_arrives(dist)
            share([(dist, 0), (-dist, 0)] if dist < 4 else [(4, 0)])
        elif what[1] == "b":
            _, _, item, step = what
            b_arrives(item, step)
            share([(item, -step), (item, step)] if step < 4 else [(item, 4)])
        elif what[1] == "w":
            h = what[2]
            take(one_r.at[h])
            for way in range(2):
                y_send(way, 1, 1, h)
        else:
            kind, step, h = (0 if what[1] == "o" else 1), what[2], what[3]
            ways = [way for way in range(2) if step <= y_steps(way, kind)]
            take(y_sem(kind, step, h), len(ways))
            for way in ways:
                if step < y_steps(way, kind):
                    y_send(way, kind, step + 1, h)
        take_shared(False)

    def tokens_of(q, count):
        def stack(parts):
            return jnp.concatenate(parts, axis=0)

        return jnp.concatenate(
            [
                stack([tb[q + i, 0:64, :] for i in range(count)]),
                stack([tb[q + i, 64:128, :] for i in range(count)]),
                stack([tail[q + i, :, 0:96] for i in range(count)]),
            ],
            axis=1,
        )

    def forward(m, cc, acc):
        for j in range(4):
            w = jnp.concatenate([wb[cc, 4 * j + i] for i in range(4)], axis=1)
            acc += jnp.dot(w, tokens_of((m * 2 + cc) * 32 + 8 * j, 8), preferred_element_type=F32)
        return acc

    accs = [forward(m, core, jnp.zeros((ROWS, TOK), F32)) for m in range(2)]
    take_shared(True)
    accs = [forward(m, 1 - core, accs[m]) for m in range(2)]
    copy(cot_send, ct.at[1 - z_lo], 2, one_r.at[2], partner).wait_recv()
    for m in range(2):
        acc = accs[m]
        for t in range(3):
            wide = min(128, TOK - 128 * t)
            both[t, :, 0:wide] = acc[:, 128 * t : 128 * t + wide]
        for t in range(3):
            wide = min(128, TOK - 128 * t)
            gate = both[t, pl.ds(0, HALF, stride=2), :][:, 0:wide]
            up = both[t, pl.ds(1, HALF, stride=2), :][:, 0:wide]
            cot = ct[m, :, 128 * t : 128 * t + wide].astype(F32)[0:HALF]
            sig = jax.nn.sigmoid(gate)
            silu = gate * sig
            hid = jnp.concatenate([silu * up, jnp.zeros((8, wide), F32)], axis=0)
            hb[m, :, 128 * t : 128 * t + wide] = hid.astype(BF16)
            both[t, pl.ds(0, HALF, stride=2), 0:wide] = cot * up * sig * (1.0 + gate * (1.0 - sig))
            both[t, pl.ds(1, HALF, stride=2), 0:wide] = cot * silu
            dbt[m, :, 128 * t : 128 * t + wide] = both[t, :, 0:wide].astype(BF16)

    def partial(offset, kind, h):
        rows = row_block(kind, offset)
        total = jnp.zeros((ROWS, 128), F32)
        for m in range(2):
            total += lax.dot_general(
                dbt[m], tokens_of((m * 2 + h) * 32 + 2 * rows, 2), (((1,), (1,)), ((), ())), preferred_element_type=F32
            )
        return total

    order = {}
    for way in range(2):
        for kind in range(2):
            for step in range(1, y_steps(way, kind) + 1):
                for h in range(2):
                    order[way, kind, step, h] = len(order)

    def g_copy(way, kind, step, h):
        k = order[way, kind, step, h]
        to = on_y_partner if kind == 1 and step == y_steps(way, kind) else on_y
        return copy(rs_send.at[k], rs_recv.at[k], 1, g_r.at[k], to(1 - 2 * way))

    def arrived(way, kind, step, h):
        g_copy(way, kind, step, h).wait_recv()
        return rs_recv[order[way, kind, step, h]].astype(F32)

    def hop(way, kind, step, h):
        steps = y_steps(way, kind)
        total = partial((1 - 2 * way) * (steps + 1 - step), kind, h)
        if step > 1:
            total += arrived(way, kind, step - 1, h)
        rs_send[order[way, kind, step, h]] = total.astype(BF16)
        start(g_copy(way, kind, step, h), 1)

    def fin_copy(h):
        return copy(fin_send.at[h], fin_recv.at[h], 1, one_r.at[4 + h], partner)

    up_order = [(kind, step, h) for step in range(1, 5) for kind in (0, 1) for h in (0, 1) if step <= y_steps(0, kind)]
    down_order = [(kind, step, h) for step in range(1, 3) for kind in (1, 0) for h in (0, 1)]
    down_order += [(1, 3, 0), (1, 3, 1), (0, 3, 0), (1, 4, 0), (1, 4, 1), (0, 3, 1)]
    for slot in range(14):
        hop(1, *down_order[slot])
        hop(0, *up_order[slot])
        if slot == 1:
            start(copy(hb.at[1 - z_lo], hid_recv, 3, one_r.at[3], partner), 3)
        if slot in (4, 5):
            fin_send[slot - 4] = partial(0, 1, slot - 4).astype(BF16)
            start(fin_copy(slot - 4), 1)
        if slot == 7:
            copy(hb.at[1 - z_lo], hid_recv, 3, one_r.at[3], partner).wait_recv()
            here = hb[z_lo].astype(F32)
            there = hid_recv[...].astype(F32)
            h_low = jnp.where(z_lo == 0, here, there)[0:HALF]
            h_high = jnp.where(z_lo == 0, there, here)[0 : HID - HALF]
            hid_keep[...] = jnp.concatenate([h_low, h_high], axis=0).astype(BF16)
            hid_copy = pltpu.make_async_copy(hid_keep, hid_out, out_sem.at[0])
            hid_copy.start()

    def put(parts, is_low):
        rows = jnp.concatenate(
            [parts[0][:, 0:64], parts[1][:, 0:64], parts[0][:, 64:128], parts[1][:, 64:128]], axis=1
        )

        rows = rows.reshape(HALF, 2, KB)

        @pl.when(is_low)
        def _():
            grad[0:HALF] = rows
            grad_copies[0].start()

        @pl.when(jnp.logical_not(is_low))
        def _():
            grad[HALF:HID] = rows[0 : HID - HALF]
            grad_copies[1].start()

    grad_copies = [
        pltpu.make_async_copy(grad.at[pl.ds(lo, n)], grad_out.at[pl.ds(lo, n)], out_sem.at[k])
        for k, lo, n in ((1, 0, HALF), (2, HALF, HID - HALF))
    ]
    own_terms = [partial(0, 0, h) for h in range(2)]
    others = []
    for h in range(2):
        fin_copy(h).wait_recv()
        others.append(fin_recv[h].astype(F32) + arrived(0, 1, 3, h) + arrived(1, 1, 4, h))
    put(others, z_lo == 1)
    put([own_terms[h] + arrived(1, 0, 3, h) + arrived(0, 0, 4, h) for h in range(2)], z_lo == 0)
    for c in grad_copies:
        c.wait()
    hid_copy.wait()
    for kind in range(2):
        all_left(kind)
    copy(cot_send, ct.at[z_lo], 2, one_r.at[2], partner).wait_send()
    copy(hb.at[1 - z_lo], hid_recv, 3, one_r.at[3], partner).wait_send()


def move(hid_in, grad_in, hid_out, grad_out, hid, grad, sem):
    arrive = [
        pltpu.make_async_copy(grad_in, grad, sem.at[0]),
        pltpu.make_async_copy(hid_in, hid, sem.at[1]),
    ]
    leave = [
        pltpu.make_async_copy(grad, grad_out, sem.at[2]),
        pltpu.make_async_copy(hid, hid_out, sem.at[3]),
    ]
    for c in arrive:
        c.start()
    for k in range(2):
        arrive[k].wait()
        leave[k].start()
    for c in leave:
        c.wait()


def body(tokens, codes, scales, cotangent):
    dma = pltpu.SemaphoreType.DMA
    hbm = pl.BlockSpec(memory_space=pltpu.HBM)
    out_shape = (jax.ShapeDtypeStruct((HID, TOK), BF16), jax.ShapeDtypeStruct((HID, 2, KB), F32))
    results = pl.pallas_call(
        kernel,
        name="glu",
        out_shape=out_shape,
        in_specs=[hbm] * 4,
        out_specs=(hbm, hbm),
        scratch_shapes=[
            pltpu.VMEM((FEAT, TOK), BF16),
            pltpu.VMEM((2 * HALF, 2, KB), BF16),
            pltpu.VMEM((2, KB), BF16),
            pltpu.VMEM((HID, TOK), BF16),
            pltpu.VMEM((128, BLOCK, 128), BF16),
            pltpu.VMEM((128, FEAT, 128), BF16),
            pltpu.VMEM((2, 16, ROWS, 128), BF16),
            pltpu.VMEM((2, ROWS, 128), BF16),
            pltpu.VMEM((2, 96, TOK), BF16),
            pltpu.VMEM((96, TOK), BF16),
            pltpu.VMEM((2, 96, TOK), BF16),
            pltpu.VMEM((HID, TOK), BF16),
            pltpu.VMEM((96, TOK), BF16),
            pltpu.VMEM((3, ROWS, 128), F32),
            pltpu.VMEM((2, ROWS, TOK), BF16),
            pltpu.VMEM((HID, 2, KB), F32),
            pltpu.VMEM((28, ROWS, 128), BF16),
            pltpu.VMEM((28, ROWS, 128), BF16),
            pltpu.VMEM((2, ROWS, 128), BF16),
            pltpu.VMEM((2, ROWS, 128), BF16),
            dma((4,)), dma((3,)), dma((4,)), dma((4,)), dma((32,)), dma((19,)), dma((16,)), dma((6,)), dma((28,)),
        ],
        compiler_params=pltpu.CompilerParams(
            collective_id=0, has_side_effects=True, vmem_limit_bytes=56 * 2**20
        ),
    )(jnp.transpose(tokens), jnp.transpose(codes, (2, 1, 0)), jnp.transpose(scales), jnp.transpose(cotangent))
    hidden, grads = pl.pallas_call(
        move,
        name="move",
        out_shape=out_shape,
        in_specs=[hbm] * 2,
        out_specs=(hbm, hbm),
        scratch_shapes=[pltpu.VMEM((HID, TOK), BF16), pltpu.VMEM((HID, 2, KB), F32), dma((4,))],
        compiler_params=pltpu.CompilerParams(vmem_limit_bytes=56 * 2**20),
    )(*results)
    return jnp.transpose(hidden), jnp.transpose(grads, (2, 1, 0))


def solution(mesh):
    in_specs = (P("local", "node"), P("local", None, "node"), P("local", None), P("local", "node"))
    out_specs = (P("local", "node"), P("local", None, "node"))
    return jax.shard_map(body, mesh=mesh, in_specs=in_specs, out_specs=out_specs, check_vma=False)
```

```python
import jax
import jax.numpy as jnp
from jax import lax
from jax.experimental import pallas as pl
from jax.experimental.pallas import tpu as pltpu
from jax.sharding import PartitionSpec as P

MESH = pl.DeviceIdType.MESH
F32 = jnp.float32
BF16 = jnp.bfloat16
TOK = 352
FEAT = 64
HID = 172
HALF = 88
ROWS = 2 * HALF
KB = 256
RING = 8
BLOCK = 176
CUT = 96

FIRST = [
    ("+", "a", 2), ("+", "a", 1), ("+", "b", 0, 1),
]
STEPS = [
    ("-", "a", 2), ("+", "a", 3), ("+", "a", 4), ("+", "b", 2, 1), ("-", "a", 1), ("+", "b", -2, 1), ("+", "b", 1, 1),
    ("+", "b", -1, 1), ("-", "b", 0, 1), ("-", "w", 0), ("+", "b", 0, 2), ("-", "w", 1), ("-", "o", 1, 0),
    ("-", "a", 3), ("+", "b", 3, 1), ("+", "b", -3, 1), ("-", "o", 1, 1), ("-", "a", 4), ("+", "b", 4, 1),
    ("-", "b", 2, 1), ("+", "b", 2, 2), ("-", "b", -2, 1), ("+", "b", -2, 2), ("-", "b", 1, 1), ("+", "b", 1, 2),
    ("-", "p", 1, 0), ("-", "b", -1, 1), ("+", "b", -1, 2), ("-", "b", 0, 2), ("+", "b", 0, 3), ("-", "p", 1, 1),
    ("-", "b", 3, 1), ("+", "b", 3, 2), ("-", "b", -3, 1), ("+", "b", -3, 2), ("-", "o", 2, 0), ("-", "b", 4, 1),
    ("+", "b", 4, 2), ("-", "b", 2, 2), ("+", "b", 2, 3), ("-", "o", 2, 1), ("-", "b", -2, 2), ("+", "b", -2, 3),
    ("-", "b", 1, 2), ("+", "b", 1, 3), ("-", "p", 2, 0), ("-", "b", -1, 2), ("+", "b", -1, 3), ("-", "b", 0, 3),
    ("+", "b", 0, 4), ("-", "p", 2, 1), ("-", "b", 3, 2), ("+", "b", 3, 3), ("-", "b", -3, 2), ("+", "b", -3, 3),
    ("-", "o", 3, 0), ("-", "b", 4, 2), ("+", "b", 4, 4), ("+", "b", 4, 3), ("-", "b", 2, 3), ("-", "o", 3, 1),
    ("+", "b", 2, 4), ("-", "b", -2, 3), ("+", "b", -2, 4), ("-", "b", 1, 3), ("+", "b", 1, 4), ("-", "p", 3, 0),
    ("-", "b", -1, 3), ("+", "b", -1, 4), ("-", "b", 0, 4), ("-", "b", 3, 3), ("+", "b", 3, 4), ("-", "p", 3, 1),
    ("-", "b", -3, 3), ("+", "b", -3, 4), ("-", "o", 4, 0), ("-", "b", 4, 4), ("-", "b", 4, 3), ("-", "b", 2, 4),
    ("-", "b", -2, 4), ("-", "o", 4, 1), ("-", "b", 1, 4), ("-", "p", 4, 0), ("-", "b", -1, 4), ("-", "b", 3, 4),
    ("-", "b", -3, 4), ("-", "p", 4, 1),
]


def kernel(
    tok_hbm, codes_hbm, scales_hbm, cot_hbm, hid_out, grad_out,
    tok, codes, scales, cots, tb, tail, wb, w_other, ct, cot_send, hb, hid_keep, hid_recv, both, dbt, grad, rs_send, rs_recv,
    fin_send, fin_recv, in_sem, out_sem, sent_sem, a_r, b_r, sib_r, y_r, one_r, g_r,
):
    loads = [
        pltpu.make_async_copy(tok_hbm, tok, in_sem.at[0]),
        pltpu.make_async_copy(codes_hbm, codes.at[pl.ds(0, HID)], in_sem.at[1]),
        pltpu.make_async_copy(scales_hbm, scales, in_sem.at[2]),
        pltpu.make_async_copy(cot_hbm, cots, in_sem.at[3]),
    ]
    for c in loads:
        c.start()

    node, local = lax.axis_index("node"), lax.axis_index("local")
    core = lax.rem(node, 2)
    x = lax.rem(lax.div(node, 2), 8)
    z_lo = lax.rem(local, 2)
    z = lax.div(node, 16) * 2 + z_lo
    y = lax.div(local, 2)

    def wrap(v):
        return lax.rem(v + RING, RING)

    def device(cx, cy, cz, cc):
        return (lax.div(cz, 2) * 16 + cx * 2 + cc, cy * 2 + lax.rem(cz, 2))

    first, second = jnp.where(core == 0, x, z), jnp.where(core == 0, z, x)

    def at(a, b):
        return jnp.where(core == 0, a, b), jnp.where(core == 0, b, a)

    def on_first(step):
        cx, cz = at(wrap(first + step), second)
        return device(cx, y, cz, core)

    def on_second(step):
        cx, cz = at(first, wrap(second + step))
        return device(cx, y, cz, core)

    def on_y(step):
        return device(x, wrap(y + step), z, core)

    sibling = device(x, y, z, 1 - core)
    other_z = lax.div(z, 2) * 2 + (1 - z_lo)
    partner = device(x, y, other_z, core)

    def on_y_partner(step):
        return device(x, wrap(y + step), other_z, core)

    def block_index(cx, cz, cc):
        return (lax.rem(cz, 2) * 2 + cc) * 32 + lax.div(cz, 2) * 8 + cx

    first_at = {a: wrap(first + a) for a in range(-4, 5)}
    second_at = {b: wrap(second + b) for b in range(-4, 5)}

    def index_of(a, b):
        cx, cz = at(first_at[a], second_at[b])
        return block_index(cx, cz, core)

    def sibling_index(a, b):
        cx, cz = at(first_at[b], second_at[a])
        return block_index(cx, cz, 1 - core)

    def block(index, part=None):
        if part is None:
            return tb.at[index]
        return tb.at[index, pl.ds(0, CUT) if part == 0 else pl.ds(CUT, BLOCK - CUT), :]

    pieces = [0, 0]

    def copy(src, dst, kind, recv_sem, target):
        return pltpu.make_async_remote_copy(
            src_ref=src, dst_ref=dst, send_sem=sent_sem.at[kind], recv_sem=recv_sem, device_id=target,
            device_id_type=MESH,
        )

    def start(c, kind, count=1):
        c.start()
        if kind < 2:
            pieces[kind] += count

    def take(recv_sem, count=1):
        ref = tb.at[pl.ds(0, count)]
        copy(ref, ref, 0, recv_sem, sibling).wait_recv()

    def all_left(kind):
        ref = tb.at[pl.ds(0, round(pieces[kind]))]
        copy(ref, ref, kind, a_r.at[0], sibling).wait_send()

    barrier = pltpu.get_barrier_semaphore()
    peers = [sibling, on_y(1), on_y(-1), on_y_partner(1), on_y_partner(-1)]
    for step in (1, -1, 2, -2):
        peers += [on_first(step), on_second(step)]
    for peer in peers:
        pl.semaphore_signal(barrier, inc=1, device_id=peer, device_id_type=MESH)

    own = index_of(0, 0)
    loads[0].wait()
    t = tok[...]
    tb[own, 0:64, :] = t[:, 0:128]
    tb[own, 64:128, :] = t[:, 128:256]
    rest = t[:, 256:352]
    tail[own, :, 0:96] = rest
    r = [rest[16 * i : 16 * i + 16, :] for i in range(4)]
    tb[own, 128:144, :] = jnp.concatenate([r[0], r[1][:, 0:32]], axis=1)
    tb[own, 144:160, :] = jnp.concatenate([r[1][:, 32:96], r[2][:, 0:64]], axis=1)
    tb[own, 160:176, :] = jnp.concatenate([r[2][:, 64:96], r[3]], axis=1)
    pl.semaphore_wait(barrier, len(peers))

    def unpack(q):
        p0, p1, p2 = tb[q, 128:144, :], tb[q, 144:160, :], tb[q, 160:176, :]
        tail[q, 0:16, 0:96] = p0[:, 0:96]
        tail[q, 16:32, 0:96] = jnp.concatenate([p0[:, 96:128], p1[:, 0:64]], axis=1)
        tail[q, 32:48, 0:96] = jnp.concatenate([p1[:, 64:128], p2[:, 0:32]], axis=1)
        tail[q, 48:64, 0:96] = p2[:, 32:128]

    def a_send(way, dist):
        sign = 1 - 2 * way
        if dist <= 2:
            at_a, hops, part = 0, dist, None
        elif dist == 3:
            at_a, hops, part = -2 * sign, 1, None
        else:
            at_a, hops, part = -2 * sign, 2, way
        ref = block(index_of(at_a, 0), part)
        start(copy(ref, ref, 0, a_r.at[dist - 1], on_first(sign * hops)), 0, share_of(dist, way))

    def share_of(step, way):
        return 1 if step < 4 else (CUT if way == 0 else BLOCK - CUT) / BLOCK

    def a_arrives(dist):
        take(a_r.at[dist - 1], 2 if dist < 4 else 1)

    def b_sem(item, step):
        return b_r.at[(item + 3) * 4 + step - 1]

    def b_send(way, item, step):
        sign = 1 - 2 * way
        hops = 2 if (item, step) == (4, 4) else 1
        ref = block(index_of(item, -sign * (step - hops)), way if step == 4 else None)
        start(copy(ref, ref, 0, b_sem(item, step), on_second(sign * hops)), 0, share_of(step, way))

    def b_arrives(item, step):
        take(b_sem(item, step), 2 if step < 4 else 1)

    shared = [[]]
    taken = [0]

    def share(blocks):
        if len(shared[-1]) == 4 or len(shared) == 1 and shared[0] == [(0, 0)]:
            shared.append([])
        for a, b in blocks:
            q = index_of(a, b)
            start(copy(block(q), block(q), 0, sib_r.at[len(shared) - 1], sibling), 0)
            shared[-1].append((a, b))
            if (a, b) != (0, 0):
                unpack(q)

    def take_shared(all_of_them):
        while taken[0] < len(shared) - (0 if all_of_them else 2):
            group = shared[taken[0]]
            take(sib_r.at[taken[0]], len(group))
            for a, b in group:
                unpack(sibling_index(a, b))
            taken[0] += 1

    def y_sem(kind, step, h):
        return y_r.at[(kind * 4 + step - 1) * 2 + h]

    def row_block(kind, offset):
        return 2 * wrap(y + offset) + (z_lo if kind == 0 else 1 - z_lo)

    def y_steps(way, kind):
        return 4 if way == kind else 3

    def y_send(way, kind, step, h):
        sign = 1 - 2 * way
        ref = wb.at[h, row_block(kind, -sign * (step - 1))]
        start(copy(ref, ref, 1, y_sem(kind, step, h), on_y(sign)), 1)

    mine = row_block(0, 0)
    theirs = row_block(1, 0)

    def w_copy(h, dst):
        return copy(w_other.at[h], wb.at[h, dst], 1, one_r.at[h], partner)

    def token_send(what):
        for way in range(2):
            if what[1] == "a":
                a_send(way, what[2])
            else:
                b_send(way, what[2], what[3])

    for what in FIRST:
        token_send(what)
    share([(0, 0)])

    codes[HID : 2 * HALF] = jnp.zeros((2 * HALF - HID, 2, KB), BF16)
    loads[1].wait()
    loads[2].wait()
    scale = scales[...].astype(F32)[None]

    def weights(half):
        part = codes[pl.ds(half * HALF, HALF)].astype(F32) * scale
        w = part.reshape(ROWS, KB).astype(BF16)
        return (
            jnp.concatenate([w[:, 0:64], w[:, 128:192]], axis=1),
            jnp.concatenate([w[:, 64:128], w[:, 192:256]], axis=1),
        )

    for h, w in enumerate(weights(1 - z_lo)):
        w_other[h] = w
        start(w_copy(h, mine), 1)
    for h, w in enumerate(weights(z_lo)):
        wb[h, mine] = w
        for way in range(2):
            y_send(way, 0, 1, h)

    loads[3].wait()
    cot = cots[...].astype(F32)
    low, high = cot[0:HALF], jnp.concatenate([cot[HALF:HID], jnp.zeros((2 * HALF - HID, TOK), F32)], axis=0)
    pad = jnp.zeros((8, TOK), F32)
    ct[z_lo] = jnp.concatenate([jnp.where(z_lo == 0, low, high), pad], axis=0).astype(BF16)
    cot_send[...] = jnp.concatenate([jnp.where(z_lo == 0, high, low), pad], axis=0).astype(BF16)

    last_send = [what for what in STEPS if what[0] == "+"][-1]
    for what in STEPS:
        if what[0] == "+":
            token_send(what)
            if what == last_send:
                start(copy(cot_send, ct.at[z_lo], 2, one_r.at[2], partner), 2)
            continue
        if what[1] == "a":
            dist = what[2]
            a_arrives(dist)
            share([(dist, 0), (-dist, 0)] if dist < 4 else [(4, 0)])
        elif what[1] == "b":
            _, _, item, step = what
            b_arrives(item, step)
            share([(item, -step), (item, step)] if step < 4 else [(item, 4)])
        elif what[1] == "w":
            h = what[2]
            take(one_r.at[h])
            for way in range(2):
                y_send(way, 1, 1, h)
        else:
            kind, step, h = (0 if what[1] == "o" else 1), what[2], what[3]
            ways = [way for way in range(2) if step <= y_steps(way, kind)]
            take(y_sem(kind, step, h), len(ways))
            for way in ways:
                if step < y_steps(way, kind):
                    y_send(way, kind, step + 1, h)
        take_shared(False)

    def tokens_of(q, count):
        def stack(parts):
            return jnp.concatenate(parts, axis=0)

        return jnp.concatenate(
            [
                stack([tb[q + i, 0:64, :] for i in range(count)]),
                stack([tb[q + i, 64:128, :] for i in range(count)]),
                stack([tail[q + i, :, 0:96] for i in range(count)]),
            ],
            axis=1,
        )

    def forward(m, cc, acc):
        for j in range(4):
            w = jnp.concatenate([wb[cc, 4 * j + i] for i in range(4)], axis=1)
            acc += jnp.dot(w, tokens_of((m * 2 + cc) * 32 + 8 * j, 8), preferred_element_type=F32)
        return acc

    accs = [forward(m, core, jnp.zeros((ROWS, TOK), F32)) for m in range(2)]
    take_shared(True)
    accs = [forward(m, 1 - core, accs[m]) for m in range(2)]
    copy(cot_send, ct.at[1 - z_lo], 2, one_r.at[2], partner).wait_recv()
    for m in range(2):
        acc = accs[m]
        for t in range(3):
            wide = min(128, TOK - 128 * t)
            both[t, :, 0:wide] = acc[:, 128 * t : 128 * t + wide]
        for t in range(3):
            wide = min(128, TOK - 128 * t)
            gate = both[t, pl.ds(0, HALF, stride=2), :][:, 0:wide]
            up = both[t, pl.ds(1, HALF, stride=2), :][:, 0:wide]
            cot = ct[m, :, 128 * t : 128 * t + wide].astype(F32)[0:HALF]
            sig = jax.nn.sigmoid(gate)
            silu = gate * sig
            hid = jnp.concatenate([silu * up, jnp.zeros((8, wide), F32)], axis=0)
            hb[m, :, 128 * t : 128 * t + wide] = hid.astype(BF16)
            both[t, pl.ds(0, HALF, stride=2), 0:wide] = cot * up * sig * (1.0 + gate * (1.0 - sig))
            both[t, pl.ds(1, HALF, stride=2), 0:wide] = cot * silu
            dbt[m, :, 128 * t : 128 * t + wide] = both[t, :, 0:wide].astype(BF16)

    def partial(offset, kind, h):
        rows = row_block(kind, offset)
        total = jnp.zeros((ROWS, 128), F32)
        for m in range(2):
            total += lax.dot_general(
                dbt[m], tokens_of((m * 2 + h) * 32 + 2 * rows, 2), (((1,), (1,)), ((), ())), preferred_element_type=F32
            )
        return total

    order = {}
    for way in range(2):
        for kind in range(2):
            for step in range(1, y_steps(way, kind) + 1):
                for h in range(2):
                    order[way, kind, step, h] = len(order)

    def g_copy(way, kind, step, h):
        k = order[way, kind, step, h]
        to = on_y_partner if kind == 1 and step == y_steps(way, kind) else on_y
        return copy(rs_send.at[k], rs_recv.at[k], 1, g_r.at[k], to(1 - 2 * way))

    def arrived(way, kind, step, h):
        g_copy(way, kind, step, h).wait_recv()
        return rs_recv[order[way, kind, step, h]].astype(F32)

    def hop(way, kind, step, h):
        steps = y_steps(way, kind)
        total = partial((1 - 2 * way) * (steps + 1 - step), kind, h)
        if step > 1:
            total += arrived(way, kind, step - 1, h)
        rs_send[order[way, kind, step, h]] = total.astype(BF16)
        start(g_copy(way, kind, step, h), 1)

    def fin_copy(h):
        return copy(fin_send.at[h], fin_recv.at[h], 1, one_r.at[4 + h], partner)

    up_order = [(kind, step, h) for step in range(1, 5) for kind in (0, 1) for h in (0, 1) if step <= y_steps(0, kind)]
    down_order = [(kind, step, h) for step in range(1, 3) for kind in (1, 0) for h in (0, 1)]
    down_order += [(1, 3, 0), (1, 3, 1), (0, 3, 0), (1, 4, 0), (1, 4, 1), (0, 3, 1)]
    for slot in range(14):
        hop(1, *down_order[slot])
        hop(0, *up_order[slot])
        if slot == 1:
            start(copy(hb.at[1 - z_lo], hid_recv, 3, one_r.at[3], partner), 3)
        if slot in (4, 5):
            fin_send[slot - 4] = partial(0, 1, slot - 4).astype(BF16)
            start(fin_copy(slot - 4), 1)
        if slot == 7:
            copy(hb.at[1 - z_lo], hid_recv, 3, one_r.at[3], partner).wait_recv()
            here = hb[z_lo].astype(F32)
            there = hid_recv[...].astype(F32)
            h_low = jnp.where(z_lo == 0, here, there)[0:HALF]
            h_high = jnp.where(z_lo == 0, there, here)[0 : HID - HALF]
            hid_keep[...] = jnp.concatenate([h_low, h_high], axis=0).astype(BF16)
            hid_copy = pltpu.make_async_copy(hid_keep, hid_out, out_sem.at[0])
            hid_copy.start()

    def put(parts, is_low):
        rows = jnp.concatenate(
            [parts[0][:, 0:64], parts[1][:, 0:64], parts[0][:, 64:128], parts[1][:, 64:128]], axis=1
        )

        rows = rows.reshape(HALF, 2, KB)

        @pl.when(is_low)
        def _():
            grad[0:HALF] = rows
            grad_copies[0].start()

        @pl.when(jnp.logical_not(is_low))
        def _():
            grad[HALF:HID] = rows[0 : HID - HALF]
            grad_copies[1].start()

    grad_copies = [
        pltpu.make_async_copy(grad.at[pl.ds(lo, n)], grad_out.at[pl.ds(lo, n)], out_sem.at[k])
        for k, lo, n in ((1, 0, HALF), (2, HALF, HID - HALF))
    ]
    own_terms = [partial(0, 0, h) for h in range(2)]
    others = []
    for h in range(2):
        fin_copy(h).wait_recv()
        others.append(fin_recv[h].astype(F32) + arrived(0, 1, 3, h) + arrived(1, 1, 4, h))
    put(others, z_lo == 1)
    put([own_terms[h] + arrived(1, 0, 3, h) + arrived(0, 0, 4, h) for h in range(2)], z_lo == 0)
    for c in grad_copies:
        c.wait()
    hid_copy.wait()
    for kind in range(2):
        all_left(kind)
    copy(cot_send, ct.at[z_lo], 2, one_r.at[2], partner).wait_send()
    copy(hb.at[1 - z_lo], hid_recv, 3, one_r.at[3], partner).wait_send()


def move(hid_in, grad_in, hid_out, grad_out, hid, grad, sem):
    arrive = [
        pltpu.make_async_copy(grad_in, grad, sem.at[0]),
        pltpu.make_async_copy(hid_in, hid, sem.at[1]),
    ]
    leave = [
        pltpu.make_async_copy(grad, grad_out, sem.at[2]),
        pltpu.make_async_copy(hid, hid_out, sem.at[3]),
    ]
    for c in arrive:
        c.start()
    for k in range(2):
        arrive[k].wait()
        leave[k].start()
    for c in leave:
        c.wait()


def body(tokens, codes, scales, cotangent):
    dma = pltpu.SemaphoreType.DMA
    hbm = pl.BlockSpec(memory_space=pltpu.HBM)
    out_shape = (jax.ShapeDtypeStruct((HID, TOK), BF16), jax.ShapeDtypeStruct((HID, 2, KB), F32))
    results = pl.pallas_call(
        kernel,
        name="glu",
        out_shape=out_shape,
        in_specs=[hbm] * 4,
        out_specs=(hbm, hbm),
        scratch_shapes=[
            pltpu.VMEM((FEAT, TOK), BF16),
            pltpu.VMEM((2 * HALF, 2, KB), BF16),
            pltpu.VMEM((2, KB), BF16),
            pltpu.VMEM((HID, TOK), BF16),
            pltpu.VMEM((128, BLOCK, 128), BF16),
            pltpu.VMEM((128, FEAT, 128), BF16),
            pltpu.VMEM((2, 16, ROWS, 128), BF16),
            pltpu.VMEM((2, ROWS, 128), BF16),
            pltpu.VMEM((2, 96, TOK), BF16),
            pltpu.VMEM((96, TOK), BF16),
            pltpu.VMEM((2, 96, TOK), BF16),
            pltpu.VMEM((HID, TOK), BF16),
            pltpu.VMEM((96, TOK), BF16),
            pltpu.VMEM((3, ROWS, 128), F32),
            pltpu.VMEM((2, ROWS, TOK), BF16),
            pltpu.VMEM((HID, 2, KB), F32),
            pltpu.VMEM((28, ROWS, 128), BF16),
            pltpu.VMEM((28, ROWS, 128), BF16),
            pltpu.VMEM((2, ROWS, 128), BF16),
            pltpu.VMEM((2, ROWS, 128), BF16),
            dma((4,)), dma((3,)), dma((4,)), dma((4,)), dma((32,)), dma((19,)), dma((16,)), dma((6,)), dma((28,)),
        ],
        compiler_params=pltpu.CompilerParams(
            collective_id=0, has_side_effects=True, vmem_limit_bytes=56 * 2**20
        ),
    )(jnp.transpose(tokens), jnp.transpose(codes, (2, 1, 0)), jnp.transpose(scales), jnp.transpose(cotangent))
    hidden, grads = pl.pallas_call(
        move,
        name="move",
        out_shape=out_shape,
        in_specs=[hbm] * 2,
        out_specs=(hbm, hbm),
        scratch_shapes=[pltpu.VMEM((HID, TOK), BF16), pltpu.VMEM((HID, 2, KB), F32), dma((4,))],
        compiler_params=pltpu.CompilerParams(vmem_limit_bytes=56 * 2**20),
    )(*results)
    return jnp.transpose(hidden), jnp.transpose(grads, (2, 1, 0))


def solution(mesh):
    in_specs = (P("local", "node"), P("local", None, "node"), P("local", None), P("local", "node"))
    out_specs = (P("local", "node"), P("local", None, "node"))
    return jax.shard_map(body, mesh=mesh, in_specs=in_specs, out_specs=out_specs, check_vma=False)
```

```python
import jax
import jax.numpy as jnp
from jax import lax
from jax.experimental import pallas as pl
from jax.experimental.pallas import tpu as pltpu
from jax.sharding import PartitionSpec as P

MESH = pl.DeviceIdType.MESH
F32 = jnp.float32
BF16 = jnp.bfloat16
TOK = 352
FEAT = 64
HID = 172
HALF = 88
ROWS = 2 * HALF
KB = 256
RING = 8
BLOCK = 176
CUT = 96

FIRST = [
    ("+", "a", 2), ("+", "a", 1), ("+", "b", 0, 1),
]
STEPS = [
    ("-", "a", 2), ("+", "a", 3), ("+", "a", 4), ("+", "b", 2, 1), ("-", "a", 1), ("+", "b", -2, 1), ("+", "b", 1, 1),
    ("+", "b", -1, 1), ("-", "b", 0, 1), ("+", "b", 0, 2), ("-", "w"),
    ("-", "a", 3), ("+", "b", 3, 1), ("+", "b", -3, 1), ("-", "o", 1), ("-", "a", 4), ("+", "b", 4, 1),
    ("-", "b", 2, 1), ("+", "b", 2, 2), ("-", "b", -2, 1), ("+", "b", -2, 2), ("-", "b", 1, 1), ("+", "b", 1, 2),
    ("-", "b", -1, 1), ("+", "b", -1, 2), ("-", "b", 0, 2), ("+", "b", 0, 3), ("-", "p", 1),
    ("-", "b", 3, 1), ("+", "b", 3, 2), ("-", "b", -3, 1), ("+", "b", -3, 2), ("-", "b", 4, 1),
    ("+", "b", 4, 2), ("-", "b", 2, 2), ("+", "b", 2, 3), ("-", "o", 2), ("-", "b", -2, 2), ("+", "b", -2, 3),
    ("-", "b", 1, 2), ("+", "b", 1, 3), ("-", "b", -1, 2), ("+", "b", -1, 3), ("-", "b", 0, 3),
    ("+", "b", 0, 4), ("-", "p", 2), ("-", "b", 3, 2), ("+", "b", 3, 3), ("-", "b", -3, 2), ("+", "b", -3, 3),
    ("-", "b", 4, 2), ("+", "b", 4, 4), ("+", "b", 4, 3), ("-", "b", 2, 3), ("-", "o", 3),
    ("+", "b", 2, 4), ("-", "b", -2, 3), ("+", "b", -2, 4), ("-", "b", 1, 3), ("+", "b", 1, 4),
    ("-", "b", -1, 3), ("+", "b", -1, 4), ("-", "b", 0, 4), ("-", "b", 3, 3), ("+", "b", 3, 4), ("-", "p", 3),
    ("-", "b", -3, 3), ("+", "b", -3, 4), ("-", "b", 4, 4), ("-", "b", 4, 3), ("-", "b", 2, 4),
    ("-", "b", -2, 4), ("-", "o", 4), ("-", "b", 1, 4), ("-", "b", -1, 4), ("-", "b", 3, 4),
    ("-", "b", -3, 4), ("-", "p", 4),
]


def kernel(
    tok_hbm, codes_hbm, scales_hbm, cot_hbm, hid_out, grad_out,
    tok, codes, scales, cots, tb, tail, wb, w_other, ct, cot_send, hb, hid_keep, hid_recv, both, dbt, grad, rs_send, rs_recv,
    fin_send, fin_recv, in_sem, out_sem, sent_sem, a_r, b_r, sib_r, y_r, one_r, g_r,
):
    loads = [
        pltpu.make_async_copy(tok_hbm, tok, in_sem.at[0]),
        pltpu.make_async_copy(codes_hbm, codes.at[pl.ds(0, HID)], in_sem.at[1]),
        pltpu.make_async_copy(scales_hbm, scales, in_sem.at[2]),
        pltpu.make_async_copy(cot_hbm, cots, in_sem.at[3]),
    ]
    for c in loads:
        c.start()

    node, local = lax.axis_index("node"), lax.axis_index("local")
    core = lax.rem(node, 2)
    x = lax.rem(lax.div(node, 2), 8)
    z_lo = lax.rem(local, 2)
    z = lax.div(node, 16) * 2 + z_lo
    y = lax.div(local, 2)

    def wrap(v):
        return lax.rem(v + RING, RING)

    def device(cx, cy, cz, cc):
        return (lax.div(cz, 2) * 16 + cx * 2 + cc, cy * 2 + lax.rem(cz, 2))

    first, second = jnp.where(core == 0, x, z), jnp.where(core == 0, z, x)

    def at(a, b):
        return jnp.where(core == 0, a, b), jnp.where(core == 0, b, a)

    def on_first(step):
        cx, cz = at(wrap(first + step), second)
        return device(cx, y, cz, core)

    def on_second(step):
        cx, cz = at(first, wrap(second + step))
        return device(cx, y, cz, core)

    def on_y(step):
        return device(x, wrap(y + step), z, core)

    sibling = device(x, y, z, 1 - core)
    other_z = lax.div(z, 2) * 2 + (1 - z_lo)
    partner = device(x, y, other_z, core)

    def on_y_partner(step):
        return device(x, wrap(y + step), other_z, core)

    def block_index(cx, cz, cc):
        return (lax.rem(cz, 2) * 2 + cc) * 32 + lax.div(cz, 2) * 8 + cx

    first_at = {a: wrap(first + a) for a in range(-4, 5)}
    second_at = {b: wrap(second + b) for b in range(-4, 5)}

    def index_of(a, b):
        cx, cz = at(first_at[a], second_at[b])
        return block_index(cx, cz, core)

    def sibling_index(a, b):
        cx, cz = at(first_at[b], second_at[a])
        return block_index(cx, cz, 1 - core)

    def block(index, part=None):
        if part is None:
            return tb.at[index]
        return tb.at[index, pl.ds(0, CUT) if part == 0 else pl.ds(CUT, BLOCK - CUT), :]

    pieces = [0, 0]

    def copy(src, dst, kind, recv_sem, target):
        return pltpu.make_async_remote_copy(
            src_ref=src, dst_ref=dst, send_sem=sent_sem.at[kind], recv_sem=recv_sem, device_id=target,
            device_id_type=MESH,
        )

    def start(c, kind, count=1):
        c.start()
        if kind < 2:
            pieces[kind] += count

    def take(recv_sem, count=1):
        ref = tb.at[pl.ds(0, count)]
        copy(ref, ref, 0, recv_sem, sibling).wait_recv()

    def all_left(kind):
        ref = tb.at[pl.ds(0, round(pieces[kind]))]
        copy(ref, ref, kind, a_r.at[0], sibling).wait_send()

    barrier = pltpu.get_barrier_semaphore()
    peers = [sibling, on_y(1), on_y(-1), on_y_partner(1), on_y_partner(-1)]
    for step in (1, -1, 2, -2):
        peers += [on_first(step), on_second(step)]
    for peer in peers:
        pl.semaphore_signal(barrier, inc=1, device_id=peer, device_id_type=MESH)

    own = index_of(0, 0)
    loads[0].wait()
    t = tok[...]
    tb[own, 0:64, :] = t[:, 0:128]
    tb[own, 64:128, :] = t[:, 128:256]
    rest = t[:, 256:352]
    tail[own, :, 0:96] = rest
    r = [rest[16 * i : 16 * i + 16, :] for i in range(4)]
    tb[own, 128:144, :] = jnp.concatenate([r[0], r[1][:, 0:32]], axis=1)
    tb[own, 144:160, :] = jnp.concatenate([r[1][:, 32:96], r[2][:, 0:64]], axis=1)
    tb[own, 160:176, :] = jnp.concatenate([r[2][:, 64:96], r[3]], axis=1)
    pl.semaphore_wait(barrier, len(peers))

    def unpack(q):
        p0, p1, p2 = tb[q, 128:144, :], tb[q, 144:160, :], tb[q, 160:176, :]
        tail[q, 0:16, 0:96] = p0[:, 0:96]
        tail[q, 16:32, 0:96] = jnp.concatenate([p0[:, 96:128], p1[:, 0:64]], axis=1)
        tail[q, 32:48, 0:96] = jnp.concatenate([p1[:, 64:128], p2[:, 0:32]], axis=1)
        tail[q, 48:64, 0:96] = p2[:, 32:128]

    def a_send(way, dist):
        sign = 1 - 2 * way
        if dist <= 2:
            at_a, hops, part = 0, dist, None
        elif dist == 3:
            at_a, hops, part = -2 * sign, 1, None
        else:
            at_a, hops, part = -2 * sign, 2, way
        ref = block(index_of(at_a, 0), part)
        start(copy(ref, ref, 0, a_r.at[dist - 1], on_first(sign * hops)), 0, share_of(dist, way))

    def share_of(step, way):
        return 1 if step < 4 else (CUT if way == 0 else BLOCK - CUT) / BLOCK

    def a_arrives(dist):
        take(a_r.at[dist - 1], 2 if dist < 4 else 1)

    def b_sem(item, step):
        return b_r.at[(item + 3) * 4 + step - 1]

    def b_send(way, item, step):
        sign = 1 - 2 * way
        hops = 2 if (item, step) == (4, 4) else 1
        ref = block(index_of(item, -sign * (step - hops)), way if step == 4 else None)
        start(copy(ref, ref, 0, b_sem(item, step), on_second(sign * hops)), 0, share_of(step, way))

    def b_arrives(item, step):
        take(b_sem(item, step), 2 if step < 4 else 1)

    shared = [[]]
    taken = [0]

    def share(blocks):
        if len(shared[-1]) == 4 or len(shared) == 1 and shared[0] == [(0, 0)]:
            shared.append([])
        for a, b in blocks:
            q = index_of(a, b)
            start(copy(block(q), block(q), 0, sib_r.at[len(shared) - 1], sibling), 0)
            shared[-1].append((a, b))
            if (a, b) != (0, 0):
                unpack(q)

    def take_shared(all_of_them):
        while taken[0] < len(shared) - (0 if all_of_them else 2):
            group = shared[taken[0]]
            take(sib_r.at[taken[0]], len(group))
            for a, b in group:
                unpack(sibling_index(a, b))
            taken[0] += 1

    def y_sem(kind, step):
        return y_r.at[kind * 4 + step - 1]

    def row_block(kind, offset):
        return 2 * wrap(y + offset) + (z_lo if kind == 0 else 1 - z_lo)

    def y_steps(way, kind):
        return 4 if way == kind else 3

    def y_send(way, kind, step):
        sign = 1 - 2 * way
        ref = wb.at[row_block(kind, -sign * (step - 1))]
        start(copy(ref, ref, 1, y_sem(kind, step), on_y(sign)), 1, 2)

    mine = row_block(0, 0)
    theirs = row_block(1, 0)

    def w_copy(dst):
        return copy(w_other, wb.at[dst], 1, one_r.at[0], partner)

    def token_send(what):
        for way in range(2):
            if what[1] == "a":
                a_send(way, what[2])
            else:
                b_send(way, what[2], what[3])

    for what in FIRST:
        token_send(what)
    share([(0, 0)])

    codes[HID : 2 * HALF] = jnp.zeros((2 * HALF - HID, 2, KB), BF16)
    loads[1].wait()
    loads[2].wait()
    scale = scales[...].astype(F32)[None]

    def weights(half):
        part = codes[pl.ds(half * HALF, HALF)].astype(F32) * scale
        w = part.reshape(ROWS, KB).astype(BF16)
        return (
            jnp.concatenate([w[:, 0:64], w[:, 128:192]], axis=1),
            jnp.concatenate([w[:, 64:128], w[:, 192:256]], axis=1),
        )

    for h, w in enumerate(weights(1 - z_lo)):
        w_other[h] = w
    start(w_copy(mine), 1, 2)
    for h, w in enumerate(weights(z_lo)):
        wb[mine, h] = w
    for way in range(2):
        y_send(way, 0, 1)

    loads[3].wait()
    cot = cots[...].astype(F32)
    low, high = cot[0:HALF], jnp.concatenate([cot[HALF:HID], jnp.zeros((2 * HALF - HID, TOK), F32)], axis=0)
    pad = jnp.zeros((8, TOK), F32)
    ct[z_lo] = jnp.concatenate([jnp.where(z_lo == 0, low, high), pad], axis=0).astype(BF16)
    cot_send[...] = jnp.concatenate([jnp.where(z_lo == 0, high, low), pad], axis=0).astype(BF16)

    last_send = [what for what in STEPS if what[0] == "+"][-1]
    for what in STEPS:
        if what[0] == "+":
            token_send(what)
            if what == last_send:
                start(copy(cot_send, ct.at[z_lo], 2, one_r.at[2], partner), 2)
            continue
        if what[1] == "a":
            dist = what[2]
            a_arrives(dist)
            share([(dist, 0), (-dist, 0)] if dist < 4 else [(4, 0)])
        elif what[1] == "b":
            _, _, item, step = what
            b_arrives(item, step)
            share([(item, -step), (item, step)] if step < 4 else [(item, 4)])
        elif what[1] == "w":
            take(one_r.at[0], 2)
            for way in range(2):
                y_send(way, 1, 1)
        else:
            kind, step = (0 if what[1] == "o" else 1), what[2]
            ways = [way for way in range(2) if step <= y_steps(way, kind)]
            take(y_sem(kind, step), 2 * len(ways))
            for way in ways:
                if step < y_steps(way, kind):
                    y_send(way, kind, step + 1)
        take_shared(False)

    def tokens_of(q, count):
        def stack(parts):
            return jnp.concatenate(parts, axis=0)

        return jnp.concatenate(
            [
                stack([tb[q + i, 0:64, :] for i in range(count)]),
                stack([tb[q + i, 64:128, :] for i in range(count)]),
                stack([tail[q + i, :, 0:96] for i in range(count)]),
            ],
            axis=1,
        )

    def forward(m, cc, acc):
        for j in range(4):
            w = jnp.concatenate([wb[4 * j + i, cc] for i in range(4)], axis=1)
            acc += jnp.dot(w, tokens_of((m * 2 + cc) * 32 + 8 * j, 8), preferred_element_type=F32)
        return acc

    accs = [forward(m, core, jnp.zeros((ROWS, TOK), F32)) for m in range(2)]
    take_shared(True)
    accs = [forward(m, 1 - core, accs[m]) for m in range(2)]
    copy(cot_send, ct.at[1 - z_lo], 2, one_r.at[2], partner).wait_recv()
    for m in range(2):
        acc = accs[m]
        for t in range(3):
            wide = min(128, TOK - 128 * t)
            both[t, :, 0:wide] = acc[:, 128 * t : 128 * t + wide]
        for t in range(3):
            wide = min(128, TOK - 128 * t)
            gate = both[t, pl.ds(0, HALF, stride=2), :][:, 0:wide]
            up = both[t, pl.ds(1, HALF, stride=2), :][:, 0:wide]
            cot = ct[m, :, 128 * t : 128 * t + wide].astype(F32)[0:HALF]
            sig = jax.nn.sigmoid(gate)
            silu = gate * sig
            hid = jnp.concatenate([silu * up, jnp.zeros((8, wide), F32)], axis=0)
            hb[m, :, 128 * t : 128 * t + wide] = hid.astype(BF16)
            both[t, pl.ds(0, HALF, stride=2), 0:wide] = cot * up * sig * (1.0 + gate * (1.0 - sig))
            both[t, pl.ds(1, HALF, stride=2), 0:wide] = cot * silu
            dbt[m, :, 128 * t : 128 * t + wide] = both[t, :, 0:wide].astype(BF16)

    def partial(offset, kind, h):
        rows = row_block(kind, offset)
        total = jnp.zeros((ROWS, 128), F32)
        for m in range(2):
            total += lax.dot_general(
                dbt[m], tokens_of((m * 2 + h) * 32 + 2 * rows, 2), (((1,), (1,)), ((), ())), preferred_element_type=F32
            )
        return total

    order = {}
    for way in range(2):
        for kind in range(2):
            for step in range(1, y_steps(way, kind) + 1):
                for h in range(2):
                    order[way, kind, step, h] = len(order)

    def g_copy(way, kind, step, h):
        k = order[way, kind, step, h]
        to = on_y_partner if kind == 1 and step == y_steps(way, kind) else on_y
        return copy(rs_send.at[k], rs_recv.at[k], 1, g_r.at[k], to(1 - 2 * way))

    def arrived(way, kind, step, h):
        g_copy(way, kind, step, h).wait_recv()
        return rs_recv[order[way, kind, step, h]].astype(F32)

    def hop(way, kind, step, h):
        steps = y_steps(way, kind)
        total = partial((1 - 2 * way) * (steps + 1 - step), kind, h)
        if step > 1:
            total += arrived(way, kind, step - 1, h)
        rs_send[order[way, kind, step, h]] = total.astype(BF16)
        start(g_copy(way, kind, step, h), 1)

    def fin_copy(h):
        return copy(fin_send.at[h], fin_recv.at[h], 1, one_r.at[4 + h], partner)

    up_order = [(kind, step, h) for step in range(1, 5) for kind in (0, 1) for h in (0, 1) if step <= y_steps(0, kind)]
    down_order = [(kind, step, h) for step in range(1, 3) for kind in (1, 0) for h in (0, 1)]
    down_order += [(1, 3, 0), (1, 3, 1), (0, 3, 0), (1, 4, 0), (1, 4, 1), (0, 3, 1)]
    for slot in range(14):
        hop(1, *down_order[slot])
        hop(0, *up_order[slot])
        if slot == 1:
            start(copy(hb.at[1 - z_lo], hid_recv, 3, one_r.at[3], partner), 3)
        if slot in (4, 5):
            fin_send[slot - 4] = partial(0, 1, slot - 4).astype(BF16)
            start(fin_copy(slot - 4), 1)
        if slot == 7:
            copy(hb.at[1 - z_lo], hid_recv, 3, one_r.at[3], partner).wait_recv()
            here = hb[z_lo].astype(F32)
            there = hid_recv[...].astype(F32)
            h_low = jnp.where(z_lo == 0, here, there)[0:HALF]
            h_high = jnp.where(z_lo == 0, there, here)[0 : HID - HALF]
            hid_keep[...] = jnp.concatenate([h_low, h_high], axis=0).astype(BF16)
            hid_copy = pltpu.make_async_copy(hid_keep, hid_out, out_sem.at[0])
            hid_copy.start()

    def put(parts, is_low):
        rows = jnp.concatenate(
            [parts[0][:, 0:64], parts[1][:, 0:64], parts[0][:, 64:128], parts[1][:, 64:128]], axis=1
        )

        rows = rows.reshape(HALF, 2, KB)

        @pl.when(is_low)
        def _():
            grad[0:HALF] = rows
            grad_copies[0].start()

        @pl.when(jnp.logical_not(is_low))
        def _():
            grad[HALF:HID] = rows[0 : HID - HALF]
            grad_copies[1].start()

    grad_copies = [
        pltpu.make_async_copy(grad.at[pl.ds(lo, n)], grad_out.at[pl.ds(lo, n)], out_sem.at[k])
        for k, lo, n in ((1, 0, HALF), (2, HALF, HID - HALF))
    ]
    own_terms = [partial(0, 0, h) for h in range(2)]
    others = []
    for h in range(2):
        fin_copy(h).wait_recv()
        others.append(fin_recv[h].astype(F32) + arrived(0, 1, 3, h) + arrived(1, 1, 4, h))
    put(others, z_lo == 1)
    put([own_terms[h] + arrived(1, 0, 3, h) + arrived(0, 0, 4, h) for h in range(2)], z_lo == 0)
    for c in grad_copies:
        c.wait()
    hid_copy.wait()
    for kind in range(2):
        all_left(kind)
    copy(cot_send, ct.at[z_lo], 2, one_r.at[2], partner).wait_send()
    copy(hb.at[1 - z_lo], hid_recv, 3, one_r.at[3], partner).wait_send()


def move(hid_in, grad_in, hid_out, grad_out, hid, grad, sem):
    arrive = [
        pltpu.make_async_copy(grad_in, grad, sem.at[0]),
        pltpu.make_async_copy(hid_in, hid, sem.at[1]),
    ]
    leave = [
        pltpu.make_async_copy(grad, grad_out, sem.at[2]),
        pltpu.make_async_copy(hid, hid_out, sem.at[3]),
    ]
    for c in arrive:
        c.start()
    for k in range(2):
        arrive[k].wait()
        leave[k].start()
    for c in leave:
        c.wait()


def body(tokens, codes, scales, cotangent):
    dma = pltpu.SemaphoreType.DMA
    hbm = pl.BlockSpec(memory_space=pltpu.HBM)
    out_shape = (jax.ShapeDtypeStruct((HID, TOK), BF16), jax.ShapeDtypeStruct((HID, 2, KB), F32))
    results = pl.pallas_call(
        kernel,
        name="glu",
        out_shape=out_shape,
        in_specs=[hbm] * 4,
        out_specs=(hbm, hbm),
        scratch_shapes=[
            pltpu.VMEM((FEAT, TOK), BF16),
            pltpu.VMEM((2 * HALF, 2, KB), BF16),
            pltpu.VMEM((2, KB), BF16),
            pltpu.VMEM((HID, TOK), BF16),
            pltpu.VMEM((128, BLOCK, 128), BF16),
            pltpu.VMEM((128, FEAT, 128), BF16),
            pltpu.VMEM((16, 2, ROWS, 128), BF16),
            pltpu.VMEM((2, ROWS, 128), BF16),
            pltpu.VMEM((2, 96, TOK), BF16),
            pltpu.VMEM((96, TOK), BF16),
            pltpu.VMEM((2, 96, TOK), BF16),
            pltpu.VMEM((HID, TOK), BF16),
            pltpu.VMEM((96, TOK), BF16),
            pltpu.VMEM((3, ROWS, 128), F32),
            pltpu.VMEM((2, ROWS, TOK), BF16),
            pltpu.VMEM((HID, 2, KB), F32),
            pltpu.VMEM((28, ROWS, 128), BF16),
            pltpu.VMEM((28, ROWS, 128), BF16),
            pltpu.VMEM((2, ROWS, 128), BF16),
            pltpu.VMEM((2, ROWS, 128), BF16),
            dma((4,)), dma((3,)), dma((4,)), dma((4,)), dma((32,)), dma((19,)), dma((8,)), dma((6,)), dma((28,)),
        ],
        compiler_params=pltpu.CompilerParams(
            collective_id=0, has_side_effects=True, vmem_limit_bytes=56 * 2**20
        ),
    )(jnp.transpose(tokens), jnp.transpose(codes, (2, 1, 0)), jnp.transpose(scales), jnp.transpose(cotangent))
    hidden, grads = pl.pallas_call(
        move,
        name="move",
        out_shape=out_shape,
        in_specs=[hbm] * 2,
        out_specs=(hbm, hbm),
        scratch_shapes=[pltpu.VMEM((HID, TOK), BF16), pltpu.VMEM((HID, 2, KB), F32), dma((4,))],
        compiler_params=pltpu.CompilerParams(vmem_limit_bytes=56 * 2**20),
    )(*results)
    return jnp.transpose(hidden), jnp.transpose(grads, (2, 1, 0))


def solution(mesh):
    in_specs = (P("local", "node"), P("local", None, "node"), P("local", None), P("local", "node"))
    out_specs = (P("local", "node"), P("local", None, "node"))
    return jax.shard_map(body, mesh=mesh, in_specs=in_specs, out_specs=out_specs, check_vma=False)
```
